512 devices in a mesh: row: 16 (over x, y_hi, core), col: 32 (over y_lo, z).
Axes of the slice: x: 4, y: 8 (y_hi: 2, y_lo: 4; y = y_hi * 4 + y_lo), z: 8, core: 2. Of those that a mesh axis runs over, the one named last changes fastest.
Arguments:
- points: bfloat16 [16384, 256], P(('row', 'col')), may hold values from -6 to 6
- basis: float32 [16384, 64], P(('row', 'col')), may hold values from -6 to 6
Outputs:
- basis_out: float32 [16384, 64], P(('row', 'col'))
- degree: float32 [16384], P(('row', 'col'))
The draws below stay inside these ranges and needn't reach their ends.
All inputs are finite; a program needn't handle non-finite values.
Results may differ from the reference program's by a relative error of at most 0.0003.
Values may be sent and summed in bfloat16 or wider, within the bound.
No kernel may reach another device: no remote copies, remote signals or barrier semaphores. Data moves between devices by JAX's collectives and lax.ppermute only.
A program may use at most 64 MiB of HBM per device.

```python
import jax
import jax.numpy as jnp
from jax import lax

F = 256
K = 64
ITERS = 2
N = 16384


def draw_points(key, part):
    key = jax.random.fold_in(key, 11)
    key_label, key_center, key_noise = jax.random.split(key, 3)
    labels = jax.random.randint(key_label, (N,), 0, 128)
    centers = jax.random.normal(key_center, (128, F), jnp.float32)
    noise = 0.5 * jax.random.normal(key_noise, (N, F), jnp.float32)
    values = jnp.clip(centers[labels] + noise, -6.0, 6.0)
    return values.astype(jnp.bfloat16)


def block_levels(stream_key, dims, cuts, least, largest):
    level, own = 1.0, jax.random.fold_in(stream_key, 6)
    for dim, blocks in cuts:
        steps = jnp.exp(jax.random.uniform(jax.random.fold_in(own, dim), (blocks,), jnp.float32, least / len(cuts), largest / len(cuts)))
        level = level * jnp.repeat(steps, dims[dim] // blocks).reshape([-1 if axis == dim else 1 for axis in range(len(dims))])
    return level


def scatter_about(stream_key, dims, deviation, reach, pieces=(), kind=jnp.bfloat16):
    level = block_levels(stream_key, dims, pieces, -0.22, 0.18) if pieces else 1.0
    result = jax.random.normal(stream_key, dims, jnp.float32) * deviation * level
    return jnp.minimum(jnp.maximum(result, -reach), reach).astype(kind)


def setup_inputs(seed: int = 0) -> dict:
    seeds = jax.random.split(jax.random.key(seed), 3)
    points = draw_points(jax.random.fold_in(seeds[2], 71), 0)
    basis = scatter_about(seeds[1], (N, K), 1.0, 6.0, ((0, 512),), jnp.float32)
    return dict(points=points, basis=basis)


def affinity(rows_blk, rows_sq, cols_pts, cols_sq, width):
    dots = lax.dot_general(rows_blk.astype(jnp.float32), cols_pts.astype(jnp.float32), (((1,), (1,)), ((), ())), preferred_element_type=jnp.float32)
    dist = rows_sq[:, None] + cols_sq[None, :] - 2.0 * dots
    return jnp.exp(-dist / (0.25 * width))

def reference(points, basis):
    count, width = points.shape
    floats = points.astype(jnp.float32)
    squares = lax.optimization_barrier(jnp.sum(floats * floats, axis=1))
    block = min(512, count)
    nblocks = count // block
    blocks = points.reshape(nblocks, block, width)
    sq_blocks = squares.reshape(nblocks, block)
    order = jnp.arange(nblocks, dtype=jnp.int32)

    def tile(index):
        return affinity(blocks[index], sq_blocks[index], points, squares, width)
    degree = lax.map(lambda index: lax.optimization_barrier(jnp.sum(tile(index), axis=1)), order).reshape(count)
    inv_root = lax.rsqrt(degree)
    for step in range(ITERS):
        scaled = basis * inv_root[:, None]
        product = lax.map(lambda index: jnp.dot(tile(index), scaled, precision=lax.Precision.HIGHEST), order)
        update = product.reshape(count, -1) * inv_root[:, None]
        gram = jnp.dot(update.T, update, precision=lax.Precision.HIGHEST)
        factor = jnp.linalg.cholesky(gram)
        basis = jax.scipy.linalg.solve_triangular(factor, update.T, lower=True).T
    return (basis, degree)
```

```python
import functools
import math

import jax
import jax.numpy as jnp
from jax import lax
from jax.experimental import pallas as pl
from jax.experimental.pallas import tpu as pltpu
from jax.sharding import Mesh, PartitionSpec as P

AXES = ("x", "yh", "core", "yl", "z")
SIZES = (4, 2, 2, 4, 8)
A_AXES = ("core", "yh", "yl")
B_AXES = ("x", "z")
NA, NB = 16, 32
HIGH = lax.Precision.HIGHEST
F32 = jnp.float32
VMEM = pl.BlockSpec(memory_space=pltpu.VMEM)
SMEM = pl.BlockSpec(memory_space=pltpu.SMEM)


def exchange(chunks, axes):
    return lax.all_to_all(chunks, axes, 0, 0, tiled=True)


def call(body, outs, *args, specs=None, scratch=(), name=None):
    return pl.pallas_call(
        body,
        out_shape=outs,
        in_specs=specs or [VMEM] * len(args),
        out_specs=[VMEM] * len(outs),
        scratch_shapes=list(scratch),
        compiler_params=pltpu.CompilerParams(vmem_limit_bytes=48 * 1024 * 1024),
        name=name,
    )(*args)


def fold(block):
    half = block.shape[0] // 2
    return jnp.concatenate([block[:half], block[half:]], axis=1)


def unfold(packed):
    return jnp.concatenate([packed[:, :64], packed[:, 64:]], axis=0)


def inverse_cholesky(gram):
    n = gram.shape[0]
    tiles = []
    sub = lax.broadcasted_iota(jnp.int32, (8, 128), 0)
    lane = lax.broadcasted_iota(jnp.int32, (8, 128), 1)
    for t in range(n // 8):
        eye = jnp.where(lane == sub + 8 * t + n, 1.0, 0.0).astype(F32)
        left = jnp.concatenate([gram[8 * t : 8 * t + 8], jnp.zeros((8, n), F32)], axis=1)
        tiles.append(left + eye)
    scale = [jnp.ones((8, 128), F32) for _ in tiles]
    group = 4
    for k in range(0, n, group):
        top = k // 8
        cols = [
            {t: jnp.broadcast_to(tiles[t][:, k + j : k + j + 1], (8, 128)) for t in range(top, n // 8)}
            for j in range(group)
        ]
        for j in range(group):
            r = (k + j) % 8
            pivot = jnp.broadcast_to(cols[j][top][r : r + 1], (8, 128))
            scale[top] = jnp.where(sub == r, lax.rsqrt(pivot), scale[top])
            inv = 1.0 / pivot
            row = jnp.broadcast_to(tiles[top][r : r + 1], (8, 128))
            heads = [jnp.broadcast_to(cols[i][top][r : r + 1], (8, 128)) for i in range(j + 1, group)]
            for t in range(top, n // 8):
                factor = cols[j][t] * inv
                if t == top:
                    factor = jnp.where(sub > r, factor, 0.0)
                tiles[t] = tiles[t] - factor * row
                for i in range(j + 1, group):
                    cols[i][t] = cols[i][t] - factor * heads[i - j - 1]
    out = jnp.concatenate([tile * s for tile, s in zip(tiles, scale)], axis=0)
    return out[:, n:]


def weights_kernel(rows_ref, cols_ref, basis_ref, w_ref, out_ref):
    rows, cols = rows_ref[...], cols_ref[...]
    width = rows.shape[1]
    dots = lax.dot_general(rows, cols, (((1,), (1,)), ((), ())), preferred_element_type=F32)
    rows32, cols32 = rows.astype(F32), cols.astype(F32)
    rows_sq = jnp.sum(rows32 * rows32, axis=1, keepdims=True)
    cols_sq = jnp.sum(cols32 * cols32, axis=1, keepdims=True)
    cols_sq = jnp.transpose(jnp.broadcast_to(cols_sq, (cols_sq.shape[0], 128)))[:1]
    dist = rows_sq + cols_sq - 2.0 * dots
    weights = jnp.exp(-dist / (0.25 * width))
    w_ref[...] = weights
    sums = jnp.sum(weights, axis=0, keepdims=True)
    head = jnp.concatenate([sums[:, 128 * i : 128 * i + 128] for i in range(4)] + [jnp.zeros((4, 128), F32)], axis=0)
    payload = jnp.concatenate([head, fold(basis_ref[...])], axis=0)
    for i in range(NA):
        out_ref[i] = payload


def first_kernel(me_ref, w_ref, in_ref, part_ref, dinv_ref, deg_ref, column_ref):
    head = in_ref[0, :8]
    for i in range(1, NA):
        head = head + in_ref[i, :8]
    mine = me_ref[0]
    picked = jnp.where(lax.broadcasted_iota(jnp.int32, (8, 128), 0) == mine // 4, head, 0.0)
    picked = jnp.broadcast_to(jnp.sum(picked, axis=0, keepdims=True), (8, 128))
    deg_ref[...] = pltpu.roll(picked, (128 - 32 * (mine % 4)) % 128, 1)
    turned = jnp.transpose(lax.rsqrt(head))
    column = jnp.concatenate([turned[:, i : i + 1] for i in range(4)], axis=0)
    column_ref[...] = jnp.broadcast_to(column, column_ref.shape)
    dinv_ref[...] = fold(column_ref[pl.ds(pl.multiple_of(mine * 32, 32), 32)][:, :64])
    scaled = jnp.concatenate([unfold(in_ref[i, 8:]) for i in range(NA)], axis=0) * column
    part = jnp.dot(w_ref[...], scaled, precision=HIGH, preferred_element_type=F32)
    for i in range(NB):
        part_ref[i] = fold(part[32 * i : 32 * i + 32])


def update_kernel(in_ref, dinv_ref, out_ref):
    total = in_ref[0]
    for i in range(1, NB):
        total = total + in_ref[i]
    dinv = dinv_ref[...]
    update = total * dinv
    lane = lax.broadcasted_iota(jnp.int32, (8, 128), 1)
    rider = jnp.where(lane % 64 < 32, dinv[:8], dinv[8:])
    payload = jnp.concatenate([update, rider], axis=0)
    for i in range(NB):
        out_ref[i] = payload


def second_kernel(w_ref, in_ref, out_ref):
    lane = lax.broadcasted_iota(jnp.int32, (8, 128), 1)
    low = lane % 64 < 32
    updates, scaled = [], []
    for i in range(NB):
        update, rider = in_ref[i, :16], in_ref[i, 16:]
        top = jnp.where(low, rider, pltpu.roll(rider, 32, 1))
        bottom = jnp.where(low, pltpu.roll(rider, 96, 1), rider)
        updates.append(update)
        scaled.append(unfold(update * jnp.concatenate([top, bottom], axis=0)))
    packed = jnp.concatenate(updates, axis=0)
    scaled = jnp.concatenate(scaled, axis=0)
    both = lax.dot_general(packed, packed, (((0,), (0,)), ((), ())), precision=HIGH, preferred_element_type=F32)
    gram = fold(both[:64, :64] + both[64:, 64:])
    part = lax.dot_general(w_ref[...], scaled, (((0,), (0,)), ((), ())), precision=HIGH, preferred_element_type=F32)
    for i in range(NA):
        out_ref[i, :16] = fold(part[32 * i : 32 * i + 32])
        out_ref[i, 16:] = gram


def normalize_kernel(in_ref, dinv_ref, update_ref, out_ref):
    total = in_ref[0]
    for i in range(1, NA):
        total = total + in_ref[i]
    update = unfold(total[:16] * dinv_ref[...])
    inverse = inverse_cholesky(unfold(total[16:]))
    update = lax.dot_general(update, inverse, (((1,), (1,)), ((), ())), precision=HIGH, preferred_element_type=F32)
    update_ref[...] = update
    gram = fold(lax.dot_general(update, update, (((0,), (0,)), ((), ())), precision=HIGH, preferred_element_type=F32))
    for i in range(NB):
        out_ref[i] = gram


def relay_kernel(in_ref, out_ref):
    total = in_ref[0]
    for i in range(1, NB):
        total = total + in_ref[i]
    for i in range(NA):
        out_ref[i] = total


def final_kernel(in_ref, update_ref, out_ref):
    total = in_ref[0]
    for i in range(1, NA):
        total = total + in_ref[i]
    inverse = inverse_cholesky(unfold(total))
    out_ref[...] = lax.dot_general(
        update_ref[...], inverse, (((1,), (1,)), ((), ())), precision=HIGH, preferred_element_type=F32
    )


def per_device(points, basis):
    own, width = points.shape
    shape = lambda *dims: jax.ShapeDtypeStruct(dims, F32)
    me = lax.axis_index(A_AXES).astype(jnp.int32).reshape(1)
    row_pts = exchange(jnp.broadcast_to(points[None], (NB, own, width)), B_AXES).reshape(NB * own, width)
    col_pts = exchange(jnp.broadcast_to(points[None], (NA, own, width)), A_AXES).reshape(NA * own, width)
    weights, sums = call(
        weights_kernel, [shape(NB * own, NA * own), shape(NA, 24, 128)], row_pts, col_pts, basis, name="weights"
    )
    sums = exchange(sums, A_AXES)
    part, dinv, degree = call(
        first_kernel,
        [shape(NB, 16, 128), shape(16, 128), shape(8, 128)],
        me,
        weights,
        sums,
        specs=[SMEM, VMEM, VMEM],
        scratch=[pltpu.VMEM((NA * own, 128), F32)],
        name="first_product",
    )
    part = exchange(part, B_AXES)
    (update,) = call(update_kernel, [shape(NB, 24, 128)], part, dinv, name="first_update")
    update = exchange(update, B_AXES)
    (part,) = call(second_kernel, [shape(NA, 48, 128)], weights, update, name="second_product")
    part = exchange(part, A_AXES)
    update, gram = call(normalize_kernel, [shape(own, 64), shape(NB, 32, 128)], part, dinv, name="normalize")
    gram = exchange(gram, B_AXES)
    (gram,) = call(relay_kernel, [shape(NA, 32, 128)], gram, name="relay")
    gram = exchange(gram, A_AXES)
    (out,) = call(final_kernel, [shape(own, 64)], gram, update, name="orthonormalize")
    return (out, degree[0, :own])


def solution(mesh):
    fine = Mesh(mesh.devices.reshape(SIZES), AXES)
    spec = P(AXES)
    return jax.shard_map(
        per_device,
        mesh=fine,
        in_specs=(P(AXES, None), P(AXES, None)),
        out_specs=(P(AXES, None), spec),
        check_vma=False,
    )
```

```python
import functools
import math

import jax
import jax.numpy as jnp
from jax import lax
from jax.experimental import pallas as pl
from jax.experimental.pallas import tpu as pltpu
from jax.sharding import Mesh, PartitionSpec as P

AXES = ("x", "yh", "core", "ym", "yl", "zh", "zl")
SIZES = (4, 2, 2, 2, 2, 4, 2)
A_AXES = ("x", "yl", "zl")
B_AXES = ("yh", "ym", "zh")
NA, NB = 16, 16
HIGH = lax.Precision.HIGHEST
F32 = jnp.float32
VMEM = pl.BlockSpec(memory_space=pltpu.VMEM)
SMEM = pl.BlockSpec(memory_space=pltpu.SMEM)


def exchange(chunks, axes):
    return lax.all_to_all(chunks, axes, 0, 0, tiled=True)


def call(body, outs, *args, specs=None, scratch=(), name=None):
    return pl.pallas_call(
        body,
        out_shape=outs,
        in_specs=specs or [VMEM] * len(args),
        out_specs=[VMEM] * len(outs),
        scratch_shapes=list(scratch),
        compiler_params=pltpu.CompilerParams(vmem_limit_bytes=48 * 1024 * 1024),
        name=name,
    )(*args)


def fold(block):
    half = block.shape[0] // 2
    return jnp.concatenate([block[:half], block[half:]], axis=1)


def unfold(packed):
    return jnp.concatenate([packed[:, :64], packed[:, 64:]], axis=0)


def inverse_cholesky(gram):
    n = gram.shape[0]
    tiles = []
    sub = lax.broadcasted_iota(jnp.int32, (8, 128), 0)
    lane = lax.broadcasted_iota(jnp.int32, (8, 128), 1)
    for t in range(n // 8):
        eye = jnp.where(lane == sub + 8 * t + n, 1.0, 0.0).astype(F32)
        left = jnp.concatenate([gram[8 * t : 8 * t + 8], jnp.zeros((8, n), F32)], axis=1)
        tiles.append(left + eye)
    scale = [jnp.ones((8, 128), F32) for _ in tiles]
    group = 4
    for k in range(0, n, group):
        top = k // 8
        cols = [
            {t: jnp.broadcast_to(tiles[t][:, k + j : k + j + 1], (8, 128)) for t in range(top, n // 8)}
            for j in range(group)
        ]
        for j in range(group):
            r = (k + j) % 8
            pivot = jnp.broadcast_to(cols[j][top][r : r + 1], (8, 128))
            scale[top] = jnp.where(sub == r, lax.rsqrt(pivot), scale[top])
            inv = 1.0 / pivot
            row = jnp.broadcast_to(tiles[top][r : r + 1], (8, 128))
            heads = [jnp.broadcast_to(cols[i][top][r : r + 1], (8, 128)) for i in range(j + 1, group)]
            for t in range(top, n // 8):
                factor = cols[j][t] * inv
                if t == top:
                    factor = jnp.where(sub > r, factor, 0.0)
                tiles[t] = tiles[t] - factor * row
                for i in range(j + 1, group):
                    cols[i][t] = cols[i][t] - factor * heads[i - j - 1]
    out = jnp.concatenate([tile * s for tile, s in zip(tiles, scale)], axis=0)
    return out[:, n:]


def total(ref):
    value = ref[0]
    for i in range(1, ref.shape[0]):
        value = value + ref[i]
    return value


def copies_kernel(points_ref, basis_ref, a_ref, b_ref, fold_ref):
    points = points_ref[...]
    for i in range(NA):
        a_ref[i] = points
    for i in range(NB):
        b_ref[i] = points
    fold_ref[...] = fold(basis_ref[...])


def weights_kernel(rows_ref, own_ref, other_ref, basis_ref, w_ref, out_ref):
    rows = rows_ref[...]
    width = rows.shape[1]
    rows32 = rows.astype(F32)
    rows_sq = jnp.sum(rows32 * rows32, axis=1, keepdims=True)
    heads = []
    for half, ref in enumerate((own_ref, other_ref)):
        cols = ref[...]
        count = cols.shape[0]
        dots = lax.dot_general(rows, cols, (((1,), (1,)), ((), ())), preferred_element_type=F32)
        cols32 = cols.astype(F32)
        cols_sq = jnp.sum(cols32 * cols32, axis=1, keepdims=True)
        cols_sq = jnp.transpose(jnp.broadcast_to(cols_sq, (count, 128)))[:1]
        dist = rows_sq + cols_sq - 2.0 * dots
        weights = jnp.exp(-dist / (0.25 * width))
        w_ref[:, half * count : half * count + count] = weights
        sums = jnp.sum(weights, axis=0, keepdims=True)
        heads += [sums[:, 128 * i : 128 * i + 128] for i in range(count // 128)]
    out_ref[:8] = jnp.concatenate(heads, axis=0)
    out_ref[8:] = basis_ref[...]


def share_kernel(core_ref, in_ref, out_ref):
    core = core_ref[0]
    mine, other = in_ref[core], in_ref[1 - core]
    head = mine[:8] + jnp.concatenate([other[4:8], other[:4]], axis=0)
    payload = jnp.concatenate([head, mine[8:], other[8:]], axis=0)
    for i in range(NA):
        out_ref[i] = payload


def first_kernel(me_ref, w_ref, in_ref, part_ref, dinv_ref, deg_ref, column_ref):
    head = in_ref[0, :8]
    for i in range(1, NA):
        head = head + in_ref[i, :8]
    mine = me_ref[0]
    picked = jnp.where(lax.broadcasted_iota(jnp.int32, (8, 128), 0) == mine // 4, head, 0.0)
    picked = jnp.broadcast_to(jnp.sum(picked, axis=0, keepdims=True), (8, 128))
    deg_ref[...] = pltpu.roll(picked, (128 - 32 * (mine % 4)) % 128, 1)
    turned = jnp.transpose(lax.rsqrt(head))
    column = jnp.concatenate([turned[:, i : i + 1] for i in range(8)], axis=0)
    column_ref[...] = jnp.broadcast_to(column[:512], column_ref.shape)
    dinv_ref[...] = fold(column_ref[pl.ds(pl.multiple_of(mine * 32, 32), 32)][:, :64])
    scaled = [unfold(in_ref[i, 8:24]) for i in range(NA)] + [unfold(in_ref[i, 24:]) for i in range(NA)]
    scaled = jnp.concatenate(scaled, axis=0) * column
    part = jnp.dot(w_ref[...], scaled, precision=HIGH, preferred_element_type=F32)
    for i in range(NB):
        part_ref[i] = fold(part[32 * i : 32 * i + 32])


def update_kernel(in_ref, dinv_ref, out_ref):
    dinv = dinv_ref[...]
    update = total(in_ref) * dinv
    lane = lax.broadcasted_iota(jnp.int32, (8, 128), 1)
    rider = jnp.where(lane % 64 < 32, dinv[:8], dinv[8:])
    payload = jnp.concatenate([update, rider], axis=0)
    for i in range(NB):
        out_ref[i] = payload


def outward_kernel(w_ref, in_ref, out_ref, scaled_ref):
    lane = lax.broadcasted_iota(jnp.int32, (8, 128), 1)
    low = lane % 64 < 32
    updates, scaled = [], []
    for i in range(NB):
        update, rider = in_ref[i, :16], in_ref[i, 16:]
        top = jnp.where(low, rider, pltpu.roll(rider, 32, 1))
        bottom = jnp.where(low, pltpu.roll(rider, 96, 1), rider)
        updates.append(update)
        scaled.append(unfold(update * jnp.concatenate([top, bottom], axis=0)))
    packed = jnp.concatenate(updates, axis=0)
    scaled = jnp.concatenate(scaled, axis=0)
    scaled_ref[...] = scaled
    both = lax.dot_general(packed, packed, (((0,), (0,)), ((), ())), precision=HIGH, preferred_element_type=F32)
    gram = fold(both[:64, :64] + both[64:, 64:])
    out_ref[NA] = gram[:16]
    out_ref[NA + 1] = gram[16:]
    half = w_ref.shape[1] // 2
    part = lax.dot_general(
        w_ref[:, half:], scaled, (((0,), (0,)), ((), ())), precision=HIGH, preferred_element_type=F32
    )
    for i in range(NA):
        out_ref[i] = fold(part[32 * i : 32 * i + 32])


def inward_kernel(w_ref, scaled_ref, out_ref):
    half = w_ref.shape[1] // 2
    part = lax.dot_general(
        w_ref[:, :half], scaled_ref[...], (((0,), (0,)), ((), ())), precision=HIGH, preferred_element_type=F32
    )
    for i in range(NA):
        out_ref[i] = fold(part[32 * i : 32 * i + 32])


def join_kernel(sent_ref, came_ref, part_ref, out_ref):
    top = sent_ref[NA] + came_ref[NA]
    bottom = sent_ref[NA + 1] + came_ref[NA + 1]
    for i in range(NA):
        out_ref[i, :16] = part_ref[i] + came_ref[i]
        out_ref[i, 16:32] = top
        out_ref[i, 32:] = bottom


def collect_kernel(in_ref, dinv_ref, out_ref, gram_ref):
    value = total(in_ref)
    update = value[:16] * dinv_ref[...]
    gram_ref[...] = value[16:]
    for i in range(NA):
        out_ref[i] = update


def factor_kernel(gram_ref, inverse_ref):
    inverse_ref[...] = inverse_cholesky(unfold(gram_ref[...]))


def twice(inverse):
    turned = jnp.transpose(inverse)
    none = jnp.zeros_like(turned)
    return jnp.concatenate(
        [jnp.concatenate([turned, none], axis=1), jnp.concatenate([none, turned], axis=1)], axis=0
    )


def normalize_kernel(in_ref, inverse_ref, mine_ref, update_ref, gram_ref):
    both = twice(inverse_ref[...])
    update = jnp.concatenate([in_ref[i] for i in range(NA)], axis=0)
    update = jnp.dot(update, both, precision=HIGH, preferred_element_type=F32)
    gram = lax.dot_general(update, update, (((0,), (0,)), ((), ())), precision=HIGH, preferred_element_type=F32)
    gram_ref[...] = fold(gram[:64, :64] + gram[64:, 64:])
    update_ref[...] = jnp.dot(mine_ref[0], both, precision=HIGH, preferred_element_type=F32)


def spread_kernel(in_ref, out_ref):
    gram = total(in_ref)
    for i in range(NB):
        out_ref[i] = gram


def final_kernel(in_ref, update_ref, out_ref):
    inverse = inverse_cholesky(unfold(total(in_ref)))
    out_ref[...] = lax.dot_general(
        unfold(update_ref[...]), inverse, (((1,), (1,)), ((), ())), precision=HIGH, preferred_element_type=F32
    )


def swap(value):
    return lax.ppermute(value, "core", [(0, 1), (1, 0)])


def per_device(points, basis):
    own, width = points.shape
    shape = lambda *dims: jax.ShapeDtypeStruct(dims, F32)
    core = lax.axis_index("core").astype(jnp.int32).reshape(1)
    me = lax.axis_index(A_AXES).astype(jnp.int32).reshape(1)
    near, far, basis = call(
        copies_kernel,
        [jax.ShapeDtypeStruct((n, own, width), points.dtype) for n in (NA, NB)] + [shape(16, 128)],
        points,
        basis,
        name="copies",
    )
    near = exchange(near, A_AXES).reshape(NA * own, width)
    near_other = swap(near)
    far = exchange(far, B_AXES).reshape(NB * own, width)
    weights, sums = call(
        weights_kernel,
        [shape(NB * own, 2 * NA * own), shape(24, 128)],
        far,
        near,
        near_other,
        basis,
        name="weights",
    )
    sums = lax.all_gather(sums, "core")
    (sums,) = call(share_kernel, [shape(NA, 40, 128)], core, sums, specs=[SMEM, VMEM], name="share")
    sums = exchange(sums, A_AXES)
    part, dinv, degree = call(
        first_kernel,
        [shape(NB, 16, 128), shape(16, 128), shape(8, 128)],
        me,
        weights,
        sums,
        specs=[SMEM, VMEM, VMEM],
        scratch=[pltpu.VMEM((NA * own, 128), F32)],
        name="first_product",
    )
    part = exchange(part, B_AXES)
    (update,) = call(update_kernel, [shape(NB, 24, 128)], part, dinv, name="first_update")
    update = exchange(update, B_AXES)
    sent, scaled = call(
        outward_kernel, [shape(NA + 2, 16, 128), shape(NB * own, 64)], weights, update, name="second_product_other"
    )
    came = swap(sent)
    (part,) = call(inward_kernel, [shape(NA, 16, 128)], weights, scaled, name="second_product_own")
    (part,) = call(join_kernel, [shape(NA, 48, 128)], sent, came, part, name="join")
    part = exchange(part, A_AXES)
    update, gram = call(collect_kernel, [shape(NA, 16, 128), shape(32, 128)], part, dinv, name="collect")
    (inverse,) = call(factor_kernel, [shape(64, 64)], gram, name="factor")
    everyone = exchange(update, A_AXES)
    update, gram = call(normalize_kernel, [shape(16, 128), shape(32, 128)], everyone, inverse, update, name="normalize")
    (gram,) = call(spread_kernel, [shape(NB, 32, 128)], lax.all_gather(gram, "core"), name="spread")
    gram = exchange(gram, B_AXES)
    (out,) = call(final_kernel, [shape(own, 64)], gram, update, name="orthonormalize")
    return (out, degree[0, :own])


def solution(mesh):
    fine = Mesh(mesh.devices.reshape(SIZES), AXES)
    spec = P(AXES)
    return jax.shard_map(
        per_device,
        mesh=fine,
        in_specs=(P(AXES, None), P(AXES, None)),
        out_specs=(P(AXES, None), spec),
        check_vma=False,
    )
```

```python
import jax
import jax.numpy as jnp
from jax import lax
from jax.experimental import pallas as pl
from jax.experimental.pallas import tpu as pltpu
from jax.sharding import Mesh, PartitionSpec as P

AXES = ("x", "yh", "core", "ym", "yl", "zh", "zl")
SIZES = (4, 2, 2, 2, 2, 4, 2)
A_AXES = ("x", "yl", "zl")
B_AXES = ("yh", "ym", "zh")
NA, NB = 16, 16
OWN, HALF, LINE = 32, 16, 256
HIGH = lax.Precision.HIGHEST
F32, BF16 = jnp.float32, jnp.bfloat16
VMEM = pl.BlockSpec(memory_space=pltpu.VMEM)
ANY = pl.BlockSpec(memory_space=pl.ANY)


def exchange(chunks, axes):
    return lax.all_to_all(chunks, axes, 0, 0, tiled=True)


def swap(value):
    return lax.ppermute(value, "core", [(0, 1), (1, 0)])


def call(body, outs, *args, specs=None, scratch=(), name=None):
    return pl.pallas_call(
        body,
        out_shape=outs,
        in_specs=specs or [VMEM] * len(args),
        out_specs=[VMEM] * len(outs),
        scratch_shapes=list(scratch),
        compiler_params=pltpu.CompilerParams(vmem_limit_bytes=48 * 1024 * 1024),
        name=name,
    )(*args)


def fold(block):
    half = block.shape[0] // 2
    return jnp.concatenate([block[:half], block[half:]], axis=1)


def unfold(packed):
    return jnp.concatenate([packed[:, :64], packed[:, 64:]], axis=0)


def total(ref):
    value = ref[0]
    for i in range(1, ref.shape[0]):
        value = value + ref[i]
    return value


def split(value):
    high = value.astype(BF16)
    rest = value - high.astype(F32)
    middle = rest.astype(BF16)
    return high, middle, (rest - middle.astype(F32)).astype(BF16)


def turn_out(packed):
    turned = jnp.transpose(packed)
    return jnp.concatenate([turned[:64], turned[64:]], axis=1)


def product(scaled, weights, axis):
    high, middle, low = (ref[...] for ref in weights)
    over = lambda left, right: lax.dot_general(
        left, right, (((1,), (axis,)), ((), ())), preferred_element_type=F32
    )
    top = over(scaled, high)
    part = over(scaled[:128], middle)
    return top[:64] + (top[64:128] + part[:64]) + (top[128:] + part[64:] + over(scaled[:64], low))


def turn_in(part):
    return jnp.transpose(jnp.concatenate([part[:, :LINE], part[:, LINE:]], axis=0))


def gram_of(packed):
    both = lax.dot_general(packed, packed, (((0,), (0,)), ((), ())), precision=HIGH, preferred_element_type=F32)
    return both[:64, :64] + both[64:, 64:]


def shrink(gram):
    blocks = gram[:32, :32], gram[32:, :32], gram[32:, 32:]
    rows = [jnp.concatenate([block[8 * j : 8 * j + 8] for j in range(4)], axis=1) for block in blocks]
    return jnp.concatenate(rows, axis=0)


def grow(packed):
    blocks = [
        jnp.concatenate([packed[8 * i : 8 * i + 8, 32 * j : 32 * j + 32] for j in range(4)], axis=0) for i in range(3)
    ]
    lower = jnp.concatenate(
        [
            jnp.concatenate([blocks[0], jnp.zeros((32, 32), F32)], axis=1),
            jnp.concatenate([blocks[1], blocks[2]], axis=1),
        ],
        axis=0,
    )
    return jnp.where(lax.broadcasted_iota(jnp.int32, (64, 64), 1) < 32, lower, jnp.transpose(lower))


def inverse_cholesky(gram):
    n = gram.shape[0]
    tiles = []
    sub = lax.broadcasted_iota(jnp.int32, (8, 128), 0)
    lane = lax.broadcasted_iota(jnp.int32, (8, 128), 1)
    for t in range(n // 8):
        eye = jnp.where(lane == sub + 8 * t + n, 1.0, 0.0).astype(F32)
        left = jnp.concatenate([gram[8 * t : 8 * t + 8], jnp.zeros((8, n), F32)], axis=1)
        tiles.append(left + eye)
    scale = [jnp.ones((8, 128), F32) for _ in tiles]
    for top in range(n // 8):
        cols = [
            {t: jnp.broadcast_to(tiles[t][:, 8 * top + j : 8 * top + j + 1], (8, 128)) for t in range(top, n // 8)}
            for j in range(8)
        ]
        for r in range(8):
            pivot = jnp.broadcast_to(cols[r][top][r : r + 1], (8, 128))
            scale[top] = jnp.where(sub == r, lax.rsqrt(pivot), scale[top])
            inv = 1.0 / pivot
            row = jnp.broadcast_to(tiles[top][r : r + 1], (8, 128))
            heads = [jnp.broadcast_to(cols[i][top][r : r + 1], (8, 128)) for i in range(r + 1, 8)]
            for t in range(top, n // 8):
                factor = cols[r][t] * inv
                if t == top:
                    factor = jnp.where(sub > r, factor, 0.0)
                tiles[t] = tiles[t] - factor * row
                for i in range(r + 1, 8):
                    cols[i][t] = cols[i][t] - factor * heads[i - r - 1]
    out = jnp.concatenate([tile * s for tile, s in zip(tiles, scale)], axis=0)
    return out[:, n:]


def near_kernel(points_ref, out_ref):
    points = points_ref[...]
    for i in range(NA):
        out_ref[i] = points


def far_kernel(points_ref, basis_ref, after_ref, out_ref, fold_ref):
    points = points_ref[...]
    for i in range(NB):
        out_ref[i] = points
    fold_ref[...] = fold(basis_ref[...])


def affinity(far_ref, near_ref, out_refs):
    rows, cols = (
        jnp.concatenate([ref[i, h : h + HALF] for h in (0, HALF) for i in range(ref.shape[0])], axis=0)
        for ref in (far_ref, near_ref)
    )
    count, width = cols.shape
    dots = lax.dot_general(rows, cols, (((1,), (1,)), ((), ())), preferred_element_type=F32)
    rows32, cols32 = rows.astype(F32), cols.astype(F32)
    rows_sq = jnp.sum(rows32 * rows32, axis=1, keepdims=True)
    cols_sq = jnp.sum(cols32 * cols32, axis=1, keepdims=True)
    cols_sq = jnp.transpose(jnp.broadcast_to(cols_sq, (count, 128)))[:1]
    dist = rows_sq + cols_sq - 2.0 * dots
    weights = jnp.exp(-dist / (0.25 * width))
    for ref, value in zip(out_refs, split(weights)):
        ref[...] = value
    sums = jnp.sum(weights, axis=0, keepdims=True)
    return jnp.concatenate([sums[:, 128 * i : 128 * i + 128] for i in range(count // 128)], axis=0)


def own_weights_kernel(far_ref, near_ref, high_ref, middle_ref, low_ref, sums_ref):
    sums_ref[:4] = affinity(far_ref, near_ref, (high_ref, middle_ref, low_ref))


def other_weights_kernel(far_ref, near_ref, sums_ref, basis_ref, high_ref, middle_ref, low_ref, out_ref):
    sums = affinity(far_ref, near_ref, (high_ref, middle_ref, low_ref))
    out_ref[:8] = jnp.concatenate([sums_ref[:4], sums], axis=0)
    out_ref[8:] = basis_ref[...]


def share_kernel(in_ref, out_ref):
    core = lax.axis_index("core")
    mine, other = in_ref[core], in_ref[1 - core]
    head = mine[:8] + jnp.concatenate([other[4:8], other[:4]], axis=0)
    payload = jnp.concatenate([head, mine[8:], other[8:]], axis=0)
    for i in range(NA):
        out_ref[i] = payload


def first_kernel(*refs):
    own_refs, other_refs = refs[:3], refs[3:6]
    in_ref, part_ref, dinv_ref, deg_ref, dinvs_ref = refs[6:]
    head = in_ref[0, :8]
    for i in range(1, NA):
        head = head + in_ref[i, :8]
    mine = lax.axis_index(A_AXES)
    sub = lax.broadcasted_iota(jnp.int32, (8, 128), 0)
    lane = lax.broadcasted_iota(jnp.int32, (8, 128), 1)
    lines = []
    for h in range(2):
        line = jnp.sum(jnp.where(sub == 2 * h + mine // 8, head, 0.0), axis=0, keepdims=True)
        lines.append(pltpu.roll(jnp.broadcast_to(line, (8, 128)), (128 + HALF * h - HALF * (mine % 8)) % 128, 1))
    deg_ref[...] = jnp.where(lane < HALF, lines[0], lines[1])[0, :OWN]
    turned = jnp.transpose(lax.rsqrt(head))
    first = lax.broadcasted_iota(jnp.int32, (LINE, 128), 1) < 64
    scaled = []
    for side in range(2):
        columns = [
            jnp.concatenate([turned[:, 4 * side + 2 * h + i : 4 * side + 2 * h + i + 1] for i in range(2)], axis=0)
            for h in range(2)
        ]
        dinv = jnp.where(first, jnp.broadcast_to(columns[0], (LINE, 128)), jnp.broadcast_to(columns[1], (LINE, 128)))
        if side == 0:
            dinvs_ref[...] = dinv
        packed = jnp.concatenate([in_ref[i, 8 + HALF * side : 24 + HALF * side] for i in range(NA)], axis=0)
        scaled.append(turn_out(packed * dinv))
    dinv_ref[...] = dinvs_ref[pl.ds(pl.multiple_of(mine * HALF, HALF), HALF)]
    part = sum(
        product(jnp.concatenate(split(values), axis=0), weights, 1)
        for values, weights in zip(scaled, (own_refs, other_refs))
    )
    part = turn_in(part)
    for i in range(NB):
        part_ref[i] = part[HALF * i : HALF * i + HALF]


def update_kernel(in_ref, dinv_ref, out_ref):
    dinv = dinv_ref[...]
    update = total(in_ref) * dinv
    lane = lax.broadcasted_iota(jnp.int32, (8, 128), 1)
    rider = jnp.where(lane % 64 < 32, dinv[:8], dinv[8:])
    payload = jnp.concatenate([update, rider], axis=0)
    for i in range(NB):
        out_ref[i] = payload


def outward_kernel(high_ref, middle_ref, low_ref, in_ref, out_ref, scaled_ref):
    lane = lax.broadcasted_iota(jnp.int32, (8, 128), 1)
    low = lane % 64 < 32
    updates, scaled = [], []
    for i in range(NB):
        update, rider = in_ref[i, :16], in_ref[i, 16:]
        top = jnp.where(low, rider, pltpu.roll(rider, 32, 1))
        bottom = jnp.where(low, pltpu.roll(rider, 96, 1), rider)
        updates.append(update)
        scaled.append(update * jnp.concatenate([top, bottom], axis=0))
    scaled = jnp.concatenate(split(turn_out(jnp.concatenate(scaled, axis=0))), axis=0)
    scaled_ref[...] = scaled
    out_ref[LINE:] = shrink(gram_of(jnp.concatenate(updates, axis=0)))
    out_ref[:LINE] = turn_in(product(scaled, (high_ref, middle_ref, low_ref), 0))


def inward_kernel(high_ref, middle_ref, low_ref, scaled_ref, out_ref):
    out_ref[...] = turn_in(product(scaled_ref[...], (high_ref, middle_ref, low_ref), 0))


def join_kernel(sent_ref, came_ref, part_ref, out_ref):
    gram = sent_ref[LINE:] + came_ref[LINE:]
    for i in range(NA):
        here = slice(HALF * i, HALF * i + HALF)
        out_ref[i, :HALF] = part_ref[here] + came_ref[here]
        out_ref[i, HALF:] = gram


def collect_kernel(in_ref, dinv_ref, out_ref, gram_ref):
    value = total(in_ref)
    update = value[:HALF] * dinv_ref[...]
    gram_ref[...] = value[HALF:]
    for i in range(NA):
        out_ref[i] = update


def factor_kernel(gram_ref, inverse_ref):
    turned = jnp.transpose(inverse_cholesky(grow(gram_ref[...])))
    none = jnp.zeros_like(turned)
    inverse_ref[:64] = jnp.concatenate([turned, none], axis=1)
    inverse_ref[64:] = jnp.concatenate([none, turned], axis=1)


def normalize_kernel(in_ref, inverse_ref, update_ref, out_ref, updates_ref):
    inverse = inverse_ref[...]
    update = jnp.concatenate([in_ref[i] for i in range(NA)], axis=0)
    update = jnp.dot(update, inverse, precision=HIGH, preferred_element_type=F32)
    updates_ref[...] = update
    mine = lax.axis_index(A_AXES)
    update_ref[...] = updates_ref[pl.ds(pl.multiple_of(mine * HALF, HALF), HALF)]
    gram = shrink(gram_of(update))
    for i in range(NB):
        out_ref[i] = gram


def relay_kernel(in_ref, out_ref):
    out_ref[...] = total(in_ref)


def final_kernel(in_ref, update_ref, out_ref):
    inverse = inverse_cholesky(grow(total(in_ref)))
    out_ref[...] = lax.dot_general(
        unfold(update_ref[...]), inverse, (((1,), (1,)), ((), ())), precision=HIGH, preferred_element_type=F32
    )


def per_device(points, basis):
    own, width = points.shape
    shape = lambda *dims, dtype=F32: jax.ShapeDtypeStruct(dims, dtype)
    (near,) = call(near_kernel, [shape(NA, own, width, dtype=BF16)], points, name="near_copies")
    near = exchange(near, A_AXES)
    other = swap(near)
    far, basis = call(
        far_kernel,
        [shape(NB, own, width, dtype=BF16), shape(HALF, 128)],
        points,
        basis,
        near,
        specs=[VMEM, VMEM, ANY],
        name="far_copies",
    )
    far = exchange(far, B_AXES)
    parts = [shape(NB * own, NA * own, dtype=BF16)] * 3
    *own_weights, sums = call(own_weights_kernel, parts + [shape(8, 128)], far, near, name="own_weights")
    *other_weights, sums = call(
        other_weights_kernel, parts + [shape(8 + HALF, 128)], far, other, sums, basis, name="other_weights"
    )
    sums = lax.all_gather(sums, "core")
    (sums,) = call(share_kernel, [shape(NA, 8 + 2 * HALF, 128)], sums, name="share")
    sums = exchange(sums, A_AXES)
    part, dinv, degree = call(
        first_kernel,
        [shape(NB, HALF, 128), shape(HALF, 128), shape(own)],
        *own_weights,
        *other_weights,
        sums,
        scratch=[pltpu.VMEM((LINE, 128), F32)],
        name="first_product",
    )
    part = exchange(part, B_AXES)
    (update,) = call(update_kernel, [shape(NB, HALF + 8, 128)], part, dinv, name="first_update")
    update = exchange(update, B_AXES)
    sent, scaled = call(
        outward_kernel,
        [shape(LINE + 24, 128), shape(192, NB * own, dtype=BF16)],
        *other_weights,
        update,
        name="second_product_other",
    )
    came = swap(sent)
    (part,) = call(inward_kernel, [shape(LINE, 128)], *own_weights, scaled, name="second_product_own")
    (part,) = call(join_kernel, [shape(NA, HALF + 24, 128)], sent, came, part, name="join")
    part = exchange(part, A_AXES)
    update, gram = call(collect_kernel, [shape(NA, HALF, 128), shape(24, 128)], part, dinv, name="collect")
    (inverse,) = call(factor_kernel, [shape(128, 128)], gram, name="factor")
    everyone = exchange(update, A_AXES)
    update, gram = call(
        normalize_kernel,
        [shape(HALF, 128), shape(NB, 24, 128)],
        everyone,
        inverse,
        scratch=[pltpu.VMEM((LINE, 128), F32)],
        name="normalize",
    )
    (gram,) = call(relay_kernel, [shape(24, 128)], exchange(gram, B_AXES), name="relay")
    (out,) = call(final_kernel, [shape(own, 64)], lax.all_gather(gram, "core"), update, name="orthonormalize")
    return (out, degree)


def solution(mesh):
    fine = Mesh(mesh.devices.reshape(SIZES), AXES)
    return jax.shard_map(
        per_device,
        mesh=fine,
        in_specs=(P(AXES, None), P(AXES, None)),
        out_specs=(P(AXES, None), P(AXES)),
        check_vma=False,
    )
```

```python
import math

import jax
import jax.numpy as jnp
from jax import lax
from jax.experimental import pallas as pl
from jax.experimental.pallas import tpu as pltpu
from jax.sharding import Mesh, PartitionSpec as P

AXES = ("x", "yh", "core", "ym", "yl", "zh", "zl")
SIZES = (4, 2, 2, 2, 2, 4, 2)
NEAR = ("x", "yl", "zl")
FAR = ("yh", "ym", "zh")
NN, NF = 16, 16
OWN, HALF, LINE = 32, 16, 256
HIGH = lax.Precision.HIGHEST
F32, BF16 = jnp.float32, jnp.bfloat16
VMEM = pl.BlockSpec(memory_space=pltpu.VMEM)
ANY = pl.BlockSpec(memory_space=pl.ANY)


def exchange(chunks, axes):
    return lax.all_to_all(chunks, axes, 0, 0, tiled=True)


def swap(value):
    return lax.ppermute(value, "core", [(0, 1), (1, 0)])


def call(body, outs, *args, specs=None, scratch=(), name=None):
    return pl.pallas_call(
        body,
        out_shape=outs,
        in_specs=specs or [VMEM] * len(args),
        out_specs=[VMEM] * len(outs),
        scratch_shapes=list(scratch),
        compiler_params=pltpu.CompilerParams(vmem_limit_bytes=48 * 1024 * 1024),
        name=name,
    )(*args)


def fold(block):
    half = block.shape[0] // 2
    return jnp.concatenate([block[:half], block[half:]], axis=1)


def unfold(packed):
    return jnp.concatenate([packed[:, :64], packed[:, 64:]], axis=0)


def total(ref):
    value = ref[0]
    for i in range(1, ref.shape[0]):
        value = value + ref[i]
    return value


def split(value):
    high = value.astype(BF16)
    rest = value - high.astype(F32)
    middle = rest.astype(BF16)
    return high, middle, (rest - middle.astype(F32)).astype(BF16)


def turn_out(packed):
    turned = jnp.transpose(packed)
    return jnp.concatenate([turned[:64], turned[64:]], axis=1)


def product(scaled, weights, axis):
    high, middle, low = (ref[...] for ref in weights)
    over = lambda left, right: lax.dot_general(
        left, right, (((1,), (axis,)), ((), ())), preferred_element_type=F32
    )
    top = over(scaled, high)
    part = over(scaled[:128], middle)
    return top[:64] + (top[64:128] + part[:64]) + (top[128:] + part[64:] + over(scaled[:64], low))


def turn_in(part):
    return jnp.transpose(jnp.concatenate([part[:, :LINE], part[:, LINE:]], axis=0))


def gram_of(packed):
    both = lax.dot_general(packed, packed, (((0,), (0,)), ((), ())), precision=HIGH, preferred_element_type=F32)
    return both[:64, :64] + both[64:, 64:]


def shrink(gram):
    blocks = gram[:32, :32], gram[32:, :32], gram[32:, 32:]
    rows = [jnp.concatenate([block[8 * j : 8 * j + 8] for j in range(4)], axis=1) for block in blocks]
    return jnp.concatenate(rows, axis=0)


def grow(packed):
    blocks = [
        jnp.concatenate([packed[8 * i : 8 * i + 8, 32 * j : 32 * j + 32] for j in range(4)], axis=0) for i in range(3)
    ]
    lower = jnp.concatenate(
        [
            jnp.concatenate([blocks[0], jnp.zeros((32, 32), F32)], axis=1),
            jnp.concatenate([blocks[1], blocks[2]], axis=1),
        ],
        axis=0,
    )
    return jnp.where(lax.broadcasted_iota(jnp.int32, (64, 64), 1) < 32, lower, jnp.transpose(lower))


def inverse_cholesky(gram):
    n = gram.shape[0]
    tiles = []
    sub = lax.broadcasted_iota(jnp.int32, (8, 128), 0)
    lane = lax.broadcasted_iota(jnp.int32, (8, 128), 1)
    for t in range(n // 8):
        eye = jnp.where(lane == sub + 8 * t + n, 1.0, 0.0).astype(F32)
        left = jnp.concatenate([gram[8 * t : 8 * t + 8], jnp.zeros((8, n), F32)], axis=1)
        tiles.append(left + eye)
    scale = [jnp.ones((8, 128), F32) for _ in tiles]
    for top in range(n // 8):
        cols = [
            {t: jnp.broadcast_to(tiles[t][:, 8 * top + j : 8 * top + j + 1], (8, 128)) for t in range(top, n // 8)}
            for j in range(8)
        ]
        for r in range(8):
            pivot = jnp.broadcast_to(cols[r][top][r : r + 1], (8, 128))
            scale[top] = jnp.where(sub == r, lax.rsqrt(pivot), scale[top])
            inv = 1.0 / pivot
            row = jnp.broadcast_to(tiles[top][r : r + 1], (8, 128))
            heads = [jnp.broadcast_to(cols[i][top][r : r + 1], (8, 128)) for i in range(r + 1, 8)]
            for t in range(top, n // 8):
                factor = cols[r][t] * inv
                if t == top:
                    factor = jnp.where(sub > r, factor, 0.0)
                tiles[t] = tiles[t] - factor * row
                for i in range(r + 1, 8):
                    cols[i][t] = cols[i][t] - factor * heads[i - r - 1]
    out = jnp.concatenate([tile * s for tile, s in zip(tiles, scale)], axis=0)
    return out[:, n:]


def rider_of(dinv):
    lane = lax.broadcasted_iota(jnp.int32, (8, 128), 1)
    return jnp.where(lane % 64 < 32, dinv[:8], dinv[8:])


def dinv_of(rider):
    low = lax.broadcasted_iota(jnp.int32, (8, 128), 1) % 64 < 32
    top = jnp.where(low, rider, pltpu.roll(rider, 32, 1))
    return jnp.concatenate([top, jnp.where(low, pltpu.roll(rider, 96, 1), rider)], axis=0)


def near_kernel(points_ref, out_ref):
    points = points_ref[...]
    for i in range(NN):
        out_ref[i] = points


def far_kernel(points_ref, basis_ref, after_ref, out_ref, fold_ref):
    points = points_ref[...]
    for i in range(NF):
        out_ref[i] = points
    fold_ref[...] = fold(basis_ref[...])


def affinity(near_ref, far_ref, out_refs):
    rows, cols = (
        jnp.concatenate([ref[i, h : h + HALF] for h in (0, HALF) for i in range(ref.shape[0])], axis=0)
        for ref in (near_ref, far_ref)
    )
    count, width = cols.shape
    rate = math.log2(math.e) / (0.25 * width)
    dots = lax.dot_general(rows, cols, (((1,), (1,)), ((), ())), preferred_element_type=F32)
    rows32, cols32 = rows.astype(F32), cols.astype(F32)
    rows_sq = jnp.sum(rows32 * rows32, axis=1, keepdims=True) * rate
    cols_sq = jnp.sum(cols32 * cols32, axis=1, keepdims=True) * rate
    cols_sq = jnp.transpose(jnp.broadcast_to(cols_sq, (count, 128)))[:1]
    weights = jnp.exp2(dots * (2.0 * rate) - (rows_sq + cols_sq))
    for ref, value in zip(out_refs, split(weights)):
        ref[...] = value
    sums = jnp.sum(weights, axis=0, keepdims=True)
    return jnp.concatenate([sums[:, 128 * i : 128 * i + 128] for i in range(count // 128)], axis=0)


def own_weights_kernel(near_ref, far_ref, high_ref, middle_ref, low_ref, sums_ref):
    sums_ref[:4] = affinity(near_ref, far_ref, (high_ref, middle_ref, low_ref))
    sums_ref[4:] = jnp.zeros((4, 128), F32)


def other_weights_kernel(near_ref, far_ref, sums_ref, basis_ref, high_ref, middle_ref, low_ref, out_ref):
    sums = affinity(near_ref, far_ref, (high_ref, middle_ref, low_ref))
    sums = sums_ref[...] + jnp.concatenate([sums, jnp.zeros((4, 128), F32)], axis=0)
    payload = jnp.concatenate([sums, basis_ref[...]], axis=0)
    for i in range(NF):
        out_ref[i] = payload


def first_kernel(*refs):
    own_refs, other_refs = refs[:3], refs[3:6]
    in_ref, part_ref, dinv_ref, deg_ref, dinvs_ref = refs[6:]
    head = in_ref[0, :8]
    for i in range(1, NF):
        head = head + in_ref[i, :8]
    mine = lax.axis_index(FAR)
    sub = lax.broadcasted_iota(jnp.int32, (8, 128), 0)
    lane = lax.broadcasted_iota(jnp.int32, (8, 128), 1)
    lines = []
    for h in range(2):
        line = jnp.sum(jnp.where(sub == 2 * h + mine // 8, head, 0.0), axis=0, keepdims=True)
        lines.append(pltpu.roll(jnp.broadcast_to(line, (8, 128)), (128 + HALF * h - HALF * (mine % 8)) % 128, 1))
    deg_ref[...] = jnp.where(lane < HALF, lines[0], lines[1])[0, :OWN]
    turned = jnp.transpose(lax.rsqrt(head))
    columns = [
        jnp.broadcast_to(jnp.concatenate([turned[:, 2 * h + i : 2 * h + i + 1] for i in range(2)], axis=0), (LINE, 128))
        for h in range(2)
    ]
    dinv = jnp.where(lax.broadcasted_iota(jnp.int32, (LINE, 128), 1) < 64, columns[0], columns[1])
    dinvs_ref[...] = dinv
    dinv_ref[...] = dinvs_ref[pl.ds(pl.multiple_of(mine * HALF, HALF), HALF)]
    packed = jnp.concatenate([in_ref[i, 8:] for i in range(NF)], axis=0)
    scaled = jnp.concatenate(split(turn_out(packed * dinv)), axis=0)
    for side, weights in enumerate((own_refs, other_refs)):
        part = turn_in(product(scaled, weights, 1))
        for i in range(NN):
            part_ref[i, HALF * side : HALF * side + HALF] = part[HALF * i : HALF * i + HALF]


def half_kernel(in_ref, dinv_ref, out_ref):
    out_ref[: 2 * HALF] = total(in_ref)
    out_ref[2 * HALF :] = dinv_ref[...]


def update_kernel(in_ref, out_ref):
    core = lax.axis_index("core")
    mine, other = in_ref[core], in_ref[1 - core]
    own_dinv, other_dinv = mine[2 * HALF :], other[2 * HALF :]
    payload = jnp.concatenate(
        [
            (mine[:HALF] + other[HALF : 2 * HALF]) * own_dinv,
            (mine[HALF : 2 * HALF] + other[:HALF]) * other_dinv,
            rider_of(own_dinv),
            rider_of(other_dinv),
        ],
        axis=0,
    )
    for i in range(NN):
        out_ref[i] = payload


def second_kernel(*refs):
    sides = refs[:3], refs[3:6]
    in_ref, out_ref, gram_ref = refs[6:]
    grams, parts = [], []
    for side, weights in enumerate(sides):
        updates, scaled = [], []
        for i in range(NN):
            update = in_ref[i, HALF * side : HALF * side + HALF]
            rider = in_ref[i, 2 * HALF + 8 * side : 2 * HALF + 8 * side + 8]
            updates.append(update)
            scaled.append(update * dinv_of(rider))
        scaled = jnp.concatenate(split(turn_out(jnp.concatenate(scaled, axis=0))), axis=0)
        parts.append(product(scaled, weights, 0))
        grams.append(gram_of(jnp.concatenate(updates, axis=0)))
    gram_ref[...] = shrink(grams[0] + grams[1])
    gram = gram_ref[pl.ds(pl.multiple_of(lax.axis_index("core") * 8, 8), 16)]
    part = turn_in(parts[0] + parts[1])
    for i in range(NF):
        out_ref[i, :HALF] = part[HALF * i : HALF * i + HALF]
        out_ref[i, HALF:] = gram


def collect_kernel(in_ref, dinv_ref, out_ref, gram_ref):
    value = total(in_ref)
    update = value[:HALF] * dinv_ref[...]
    gram_ref[...] = value[HALF:]
    for i in range(NF):
        out_ref[i] = update


def factor_kernel(gram_ref, inverse_ref):
    gram = jnp.concatenate([gram_ref[0], gram_ref[1, 8:]], axis=0)
    turned = jnp.transpose(inverse_cholesky(grow(gram)))
    none = jnp.zeros_like(turned)
    inverse_ref[:64] = jnp.concatenate([turned, none], axis=1)
    inverse_ref[64:] = jnp.concatenate([none, turned], axis=1)


def normalize_kernel(in_ref, inverse_ref, update_ref, out_ref, updates_ref):
    update = jnp.concatenate([in_ref[i] for i in range(NF)], axis=0)
    update = jnp.dot(update, inverse_ref[...], precision=HIGH, preferred_element_type=F32)
    updates_ref[...] = update
    mine = lax.axis_index(FAR)
    update_ref[...] = updates_ref[pl.ds(pl.multiple_of(mine * HALF, HALF), HALF)]
    gram = shrink(gram_of(update))
    for i in range(NN):
        out_ref[i] = gram


def relay_kernel(in_ref, out_ref):
    out_ref[...] = total(in_ref)


def final_kernel(in_ref, update_ref, out_ref):
    inverse = inverse_cholesky(grow(total(in_ref)))
    out_ref[...] = lax.dot_general(
        unfold(update_ref[...]), inverse, (((1,), (1,)), ((), ())), precision=HIGH, preferred_element_type=F32
    )


def per_device(points, basis):
    own, width = points.shape
    shape = lambda *dims, dtype=F32: jax.ShapeDtypeStruct(dims, dtype)
    (near,) = call(near_kernel, [shape(NN, own, width, dtype=BF16)], points, name="near_copies")
    near = exchange(near, NEAR)
    other = swap(near)
    far, basis = call(
        far_kernel,
        [shape(NF, own, width, dtype=BF16), shape(HALF, 128)],
        points,
        basis,
        near,
        specs=[VMEM, VMEM, ANY],
        name="far_copies",
    )
    far = exchange(far, FAR)
    parts = [shape(NN * own, NF * own, dtype=BF16)] * 3
    *own_weights, sums = call(own_weights_kernel, parts + [shape(8, 128)], near, far, name="own_weights")
    *other_weights, sums = call(
        other_weights_kernel, parts + [shape(NF, 8 + HALF, 128)], other, far, sums, basis, name="other_weights"
    )
    weights = own_weights + other_weights
    part, dinv, degree = call(
        first_kernel,
        [shape(NN, 2 * HALF, 128), shape(HALF, 128), shape(own)],
        *weights,
        exchange(sums, FAR),
        scratch=[pltpu.VMEM((LINE, 128), F32)],
        name="first_product",
    )
    (part,) = call(half_kernel, [shape(3 * HALF, 128)], exchange(part, NEAR), dinv, name="half_update")
    (update,) = call(update_kernel, [shape(NN, 2 * HALF + 16, 128)], lax.all_gather(part, "core"), name="first_update")
    (part,) = call(
        second_kernel,
        [shape(NF, HALF + 16, 128)],
        *weights,
        exchange(update, NEAR),
        scratch=[pltpu.VMEM((24, 128), F32)],
        name="second_product",
    )
    update, gram = call(
        collect_kernel, [shape(NF, HALF, 128), shape(16, 128)], exchange(part, FAR), dinv, name="collect"
    )
    everyone = exchange(update, FAR)
    (inverse,) = call(factor_kernel, [shape(128, 128)], lax.all_gather(gram, "core"), name="factor")
    update, gram = call(
        normalize_kernel,
        [shape(HALF, 128), shape(NN, 24, 128)],
        everyone,
        inverse,
        scratch=[pltpu.VMEM((LINE, 128), F32)],
        name="normalize",
    )
    (gram,) = call(relay_kernel, [shape(24, 128)], exchange(gram, NEAR), name="relay")
    (out,) = call(final_kernel, [shape(own, 64)], lax.all_gather(gram, "core"), update, name="orthonormalize")
    return (out, degree)


def solution(mesh):
    fine = Mesh(mesh.devices.reshape(SIZES), AXES)
    return jax.shard_map(
        per_device,
        mesh=fine,
        in_specs=(P(AXES, None), P(AXES, None)),
        out_specs=(P(AXES, None), P(AXES)),
        check_vma=False,
    )
```

```python
import math

import jax
import jax.numpy as jnp
from jax import lax
from jax.experimental import pallas as pl
from jax.experimental.pallas import tpu as pltpu
from jax.sharding import Mesh, PartitionSpec as P

AXES = ("x", "yh", "core", "ym", "yl", "zh", "zl")
SIZES = (4, 2, 2, 2, 2, 4, 2)
NEAR = ("x", "yl", "zl")
FAR = ("yh", "ym", "zh")
NN, NF = 16, 16
OWN, HALF, LINE = 32, 16, 256
HIGH = lax.Precision.HIGHEST
F32, BF16 = jnp.float32, jnp.bfloat16
VMEM = pl.BlockSpec(memory_space=pltpu.VMEM)
ANY = pl.BlockSpec(memory_space=pl.ANY)


def exchange(chunks, axes):
    return lax.all_to_all(chunks, axes, 0, 0, tiled=True)


def swap(value):
    return lax.ppermute(value, "core", [(0, 1), (1, 0)])


def call(body, outs, *args, specs=None, scratch=(), name=None):
    return pl.pallas_call(
        body,
        out_shape=outs,
        in_specs=specs or [VMEM] * len(args),
        out_specs=[VMEM] * len(outs),
        scratch_shapes=list(scratch),
        compiler_params=pltpu.CompilerParams(vmem_limit_bytes=48 * 1024 * 1024),
        name=name,
    )(*args)


def fold(block):
    half = block.shape[0] // 2
    return jnp.concatenate([block[:half], block[half:]], axis=1)


def unfold(packed):
    return jnp.concatenate([packed[:, :64], packed[:, 64:]], axis=0)


def total(ref):
    value = ref[0]
    for i in range(1, ref.shape[0]):
        value = value + ref[i]
    return value


def split(value):
    high = value.astype(BF16)
    rest = value - high.astype(F32)
    middle = rest.astype(BF16)
    return high, middle, (rest - middle.astype(F32)).astype(BF16)


def turn_out(packed):
    turned = jnp.transpose(packed)
    return jnp.concatenate([turned[:64], turned[64:]], axis=1)


def product(scaled, weights, axis):
    high, middle = (ref[...] for ref in weights)
    over = lambda left, right: lax.dot_general(
        left, right, (((1,), (axis,)), ((), ())), preferred_element_type=F32
    )
    top = over(scaled, high)
    part = over(scaled[:128], middle)
    return top[:64] + (top[64:128] + part[:64]) + (top[128:] + part[64:])


def turn_in(part):
    return jnp.transpose(jnp.concatenate([part[:, :LINE], part[:, LINE:]], axis=0))


def gram_of(packed):
    both = lax.dot_general(packed, packed, (((0,), (0,)), ((), ())), precision=HIGH, preferred_element_type=F32)
    return both[:64, :64] + both[64:, 64:]


def shrink(gram):
    blocks = gram[:32, :32], gram[32:, :32], gram[32:, 32:]
    rows = [jnp.concatenate([block[8 * j : 8 * j + 8] for j in range(4)], axis=1) for block in blocks]
    return jnp.concatenate(rows, axis=0)


def grow(packed):
    blocks = [
        jnp.concatenate([packed[8 * i : 8 * i + 8, 32 * j : 32 * j + 32] for j in range(4)], axis=0) for i in range(3)
    ]
    lower = jnp.concatenate(
        [
            jnp.concatenate([blocks[0], jnp.zeros((32, 32), F32)], axis=1),
            jnp.concatenate([blocks[1], blocks[2]], axis=1),
        ],
        axis=0,
    )
    return jnp.where(lax.broadcasted_iota(jnp.int32, (64, 64), 1) < 32, lower, jnp.transpose(lower))


def inverse_cholesky(gram):
    n = gram.shape[0]
    tiles = []
    sub = lax.broadcasted_iota(jnp.int32, (8, 128), 0)
    lane = lax.broadcasted_iota(jnp.int32, (8, 128), 1)
    for t in range(n // 8):
        eye = jnp.where(lane == sub + 8 * t + n, 1.0, 0.0).astype(F32)
        left = jnp.concatenate([gram[8 * t : 8 * t + 8], jnp.zeros((8, n), F32)], axis=1)
        tiles.append(left + eye)
    scale = [jnp.ones((8, 128), F32) for _ in tiles]
    for top in range(n // 8):
        cols = [
            {t: jnp.broadcast_to(tiles[t][:, 8 * top + j : 8 * top + j + 1], (8, 128)) for t in range(top, n // 8)}
            for j in range(8)
        ]
        for r in range(8):
            pivot = jnp.broadcast_to(cols[r][top][r : r + 1], (8, 128))
            scale[top] = jnp.where(sub == r, lax.rsqrt(pivot), scale[top])
            inv = 1.0 / pivot
            row = jnp.broadcast_to(tiles[top][r : r + 1], (8, 128))
            heads = [jnp.broadcast_to(cols[i][top][r : r + 1], (8, 128)) for i in range(r + 1, 8)]
            for t in range(top, n // 8):
                factor = cols[r][t] * inv
                if t == top:
                    factor = jnp.where(sub > r, factor, 0.0)
                tiles[t] = tiles[t] - factor * row
                for i in range(r + 1, 8):
                    cols[i][t] = cols[i][t] - factor * heads[i - r - 1]
    out = jnp.concatenate([tile * s for tile, s in zip(tiles, scale)], axis=0)
    return out[:, n:]


def rider_of(dinv):
    lane = lax.broadcasted_iota(jnp.int32, (8, 128), 1)
    return jnp.where(lane % 64 < 32, dinv[:8], dinv[8:])


def dinv_of(rider):
    low = lax.broadcasted_iota(jnp.int32, (8, 128), 1) % 64 < 32
    top = jnp.where(low, rider, pltpu.roll(rider, 32, 1))
    return jnp.concatenate([top, jnp.where(low, pltpu.roll(rider, 96, 1), rider)], axis=0)


def near_kernel(points_ref, out_ref):
    points = points_ref[...]
    for i in range(NN):
        out_ref[i] = points


def far_kernel(points_ref, basis_ref, after_ref, out_ref, fold_ref):
    points = points_ref[...]
    for i in range(NF):
        out_ref[i] = points
    fold_ref[...] = fold(basis_ref[...])


def line_of(ref):
    return jnp.concatenate([ref[i, h : h + HALF] for h in (0, HALF) for i in range(ref.shape[0])], axis=0)


def squares(points, rate):
    floats = points.astype(F32)
    return jnp.sum(floats * floats, axis=1, keepdims=True) * rate


def rate_of(width):
    return math.log2(math.e) / (0.25 * width)


def line_kernel(near_ref, rows_ref, squares_ref):
    rows = line_of(near_ref)
    rows_ref[...] = rows
    squares_ref[...] = jnp.broadcast_to(squares(rows, rate_of(rows.shape[1])), squares_ref.shape)


def weights_kernel(own_ref, own_sq_ref, other_ref, other_sq_ref, far_ref, basis_ref, *refs):
    cols = line_of(far_ref)
    count, width = cols.shape
    rate = rate_of(width)
    cols_sq = jnp.transpose(jnp.broadcast_to(squares(cols, rate), (count, 128)))[:1]
    sums = []
    for rows_ref, sq_ref, high_ref, middle_ref in ((own_ref, own_sq_ref, *refs[:2]), (other_ref, other_sq_ref, *refs[2:4])):
        dots = lax.dot_general(rows_ref[...], cols, (((1,), (1,)), ((), ())), preferred_element_type=F32)
        weights = jnp.exp2(dots * (2.0 * rate) - (jnp.tile(sq_ref[...], (1, count // 128)) + cols_sq))
        high = weights.astype(BF16)
        high_ref[...] = high
        middle_ref[...] = (weights - high.astype(F32)).astype(BF16)
        sums.append(jnp.sum(weights, axis=0, keepdims=True))
    sums = sums[0] + sums[1]
    lines = [sums[:, 128 * i : 128 * i + 128] for i in range(count // 128)]
    payload = jnp.concatenate(lines + [jnp.zeros((4, 128), F32), basis_ref[...]], axis=0)
    for i in range(NF):
        refs[4][i] = payload


def first_kernel(*refs):
    own_refs, other_refs = refs[:2], refs[2:4]
    in_ref, part_ref, dinv_ref, deg_ref, dinvs_ref = refs[4:]
    head = in_ref[0, :8]
    for i in range(1, NF):
        head = head + in_ref[i, :8]
    mine = lax.axis_index(FAR)
    sub = lax.broadcasted_iota(jnp.int32, (8, 128), 0)
    lane = lax.broadcasted_iota(jnp.int32, (8, 128), 1)
    lines = []
    for h in range(2):
        line = jnp.sum(jnp.where(sub == 2 * h + mine // 8, head, 0.0), axis=0, keepdims=True)
        lines.append(pltpu.roll(jnp.broadcast_to(line, (8, 128)), (128 + HALF * h - HALF * (mine % 8)) % 128, 1))
    deg_ref[...] = jnp.where(lane < HALF, lines[0], lines[1])[0, :OWN]
    turned = jnp.transpose(lax.rsqrt(head))
    columns = [
        jnp.broadcast_to(jnp.concatenate([turned[:, 2 * h + i : 2 * h + i + 1] for i in range(2)], axis=0), (LINE, 128))
        for h in range(2)
    ]
    dinv = jnp.where(lax.broadcasted_iota(jnp.int32, (LINE, 128), 1) < 64, columns[0], columns[1])
    dinvs_ref[...] = dinv
    dinv_ref[...] = dinvs_ref[pl.ds(pl.multiple_of(mine * HALF, HALF), HALF)]
    packed = jnp.concatenate([in_ref[i, 8:] for i in range(NF)], axis=0)
    scaled = jnp.concatenate(split(turn_out(packed * dinv)), axis=0)
    for side, weights in enumerate((own_refs, other_refs)):
        part = turn_in(product(scaled, weights, 1))
        for i in range(NN):
            part_ref[i, HALF * side : HALF * side + HALF] = part[HALF * i : HALF * i + HALF]


def half_kernel(in_ref, dinv_ref, out_ref):
    out_ref[: 2 * HALF] = total(in_ref)
    out_ref[2 * HALF :] = dinv_ref[...]


def update_kernel(in_ref, out_ref):
    core = lax.axis_index("core")
    mine, other = in_ref[core], in_ref[1 - core]
    own_dinv, other_dinv = mine[2 * HALF :], other[2 * HALF :]
    payload = jnp.concatenate(
        [
            (mine[:HALF] + other[HALF : 2 * HALF]) * own_dinv,
            (mine[HALF : 2 * HALF] + other[:HALF]) * other_dinv,
            rider_of(own_dinv),
            rider_of(other_dinv),
        ],
        axis=0,
    )
    for i in range(NN):
        out_ref[i] = payload


def second_kernel(*refs):
    sides = refs[:2], refs[2:4]
    in_ref, out_ref, gram_ref = refs[4:]
    grams, parts = [], []
    for side, weights in enumerate(sides):
        updates, scaled = [], []
        for i in range(NN):
            update = in_ref[i, HALF * side : HALF * side + HALF]
            rider = in_ref[i, 2 * HALF + 8 * side : 2 * HALF + 8 * side + 8]
            updates.append(update)
            scaled.append(update * dinv_of(rider))
        scaled = jnp.concatenate(split(turn_out(jnp.concatenate(scaled, axis=0))), axis=0)
        parts.append(product(scaled, weights, 0))
        grams.append(gram_of(jnp.concatenate(updates, axis=0)))
    gram_ref[...] = shrink(grams[0] + grams[1])
    gram = gram_ref[pl.ds(pl.multiple_of(lax.axis_index("core") * 8, 8), 16)]
    part = turn_in(parts[0] + parts[1])
    for i in range(NF):
        out_ref[i, :HALF] = part[HALF * i : HALF * i + HALF]
        out_ref[i, HALF:] = gram


def collect_kernel(in_ref, dinv_ref, out_ref, gram_ref):
    value = total(in_ref)
    update = value[:HALF] * dinv_ref[...]
    gram_ref[...] = value[HALF:]
    for i in range(NF):
        out_ref[i] = update


def factor_kernel(gram_ref, inverse_ref):
    gram = jnp.concatenate([gram_ref[0], gram_ref[1, 8:]], axis=0)
    turned = jnp.transpose(inverse_cholesky(grow(gram)))
    none = jnp.zeros_like(turned)
    inverse_ref[:64] = jnp.concatenate([turned, none], axis=1)
    inverse_ref[64:] = jnp.concatenate([none, turned], axis=1)


def normalize_kernel(in_ref, inverse_ref, update_ref, out_ref, updates_ref):
    update = jnp.concatenate([in_ref[i] for i in range(NF)], axis=0)
    update = jnp.dot(update, inverse_ref[...], precision=HIGH, preferred_element_type=F32)
    updates_ref[...] = update
    mine = lax.axis_index(FAR)
    update_ref[...] = updates_ref[pl.ds(pl.multiple_of(mine * HALF, HALF), HALF)]
    gram = shrink(gram_of(update))
    for i in range(NN):
        out_ref[i] = gram


def relay_kernel(in_ref, out_ref):
    out_ref[...] = total(in_ref)


def final_kernel(in_ref, update_ref, out_ref):
    inverse = inverse_cholesky(grow(total(in_ref)))
    out_ref[...] = lax.dot_general(
        unfold(update_ref[...]), inverse, (((1,), (1,)), ((), ())), precision=HIGH, preferred_element_type=F32
    )


def per_device(points, basis):
    own, width = points.shape
    shape = lambda *dims, dtype=F32: jax.ShapeDtypeStruct(dims, dtype)
    (near,) = call(near_kernel, [shape(NN, own, width, dtype=BF16)], points, name="near_copies")
    near = exchange(near, NEAR)
    other = swap(near)
    far, basis = call(
        far_kernel,
        [shape(NF, own, width, dtype=BF16), shape(HALF, 128)],
        points,
        basis,
        near,
        specs=[VMEM, VMEM, ANY],
        name="far_copies",
    )
    far = exchange(far, FAR)
    lines = []
    for name, value in (("own", near), ("other", other)):
        lines += call(
            line_kernel, [shape(NN * own, width, dtype=BF16), shape(NN * own, 128)], value, name=name + "_line"
        )
    *weights, sums = call(
        weights_kernel,
        [shape(NN * own, NF * own, dtype=BF16)] * 4 + [shape(NF, 8 + HALF, 128)],
        *lines,
        far,
        basis,
        name="weights",
    )
    part, dinv, degree = call(
        first_kernel,
        [shape(NN, 2 * HALF, 128), shape(HALF, 128), shape(own)],
        *weights,
        exchange(sums, FAR),
        scratch=[pltpu.VMEM((LINE, 128), F32)],
        name="first_product",
    )
    (part,) = call(half_kernel, [shape(3 * HALF, 128)], exchange(part, NEAR), dinv, name="half_update")
    (update,) = call(update_kernel, [shape(NN, 2 * HALF + 16, 128)], lax.all_gather(part, "core"), name="first_update")
    (part,) = call(
        second_kernel,
        [shape(NF, HALF + 16, 128)],
        *weights,
        exchange(update, NEAR),
        scratch=[pltpu.VMEM((24, 128), F32)],
        name="second_product",
    )
    update, gram = call(
        collect_kernel, [shape(NF, HALF, 128), shape(16, 128)], exchange(part, FAR), dinv, name="collect"
    )
    everyone = exchange(update, FAR)
    (inverse,) = call(factor_kernel, [shape(128, 128)], lax.all_gather(gram, "core"), name="factor")
    update, gram = call(
        normalize_kernel,
        [shape(HALF, 128), shape(NN, 24, 128)],
        everyone,
        inverse,
        scratch=[pltpu.VMEM((LINE, 128), F32)],
        name="normalize",
    )
    (gram,) = call(relay_kernel, [shape(24, 128)], exchange(gram, NEAR), name="relay")
    (out,) = call(final_kernel, [shape(own, 64)], lax.all_gather(gram, "core"), update, name="orthonormalize")
    return (out, degree)


def solution(mesh):
    fine = Mesh(mesh.devices.reshape(SIZES), AXES)
    return jax.shard_map(
        per_device,
        mesh=fine,
        in_specs=(P(AXES, None), P(AXES, None)),
        out_specs=(P(AXES, None), P(AXES)),
        check_vma=False,
    )
```

```python
import math

import jax
import jax.numpy as jnp
from jax import lax
from jax.experimental import pallas as pl
from jax.experimental.pallas import tpu as pltpu
from jax.sharding import Mesh, PartitionSpec as P

AXES = ("x", "yh", "core", "ym", "yl", "zh", "zl")
SIZES = (4, 2, 2, 2, 2, 4, 2)
NEAR = ("x", "yl", "zl")
FAR = ("yh", "ym", "zh")
NN, NF = 16, 16
OWN, HALF, LINE = 32, 16, 256
HIGH = lax.Precision.HIGHEST
F32, BF16 = jnp.float32, jnp.bfloat16
VMEM = pl.BlockSpec(memory_space=pltpu.VMEM)
ANY = pl.BlockSpec(memory_space=pl.ANY)


def exchange(chunks, axes):
    return lax.all_to_all(chunks, axes, 0, 0, tiled=True)


def swap(value):
    return lax.ppermute(value, "core", [(0, 1), (1, 0)])


def call(body, outs, *args, specs=None, scratch=(), name=None):
    return pl.pallas_call(
        body,
        out_shape=outs,
        in_specs=specs or [VMEM] * len(args),
        out_specs=[VMEM] * len(outs),
        scratch_shapes=list(scratch),
        compiler_params=pltpu.CompilerParams(vmem_limit_bytes=48 * 1024 * 1024),
        name=name,
    )(*args)


def fold(block):
    half = block.shape[0] // 2
    return jnp.concatenate([block[:half], block[half:]], axis=1)


def unfold(packed):
    return jnp.concatenate([packed[:, :64], packed[:, 64:]], axis=0)


def total(ref):
    value = ref[0]
    for i in range(1, ref.shape[0]):
        value = value + ref[i]
    return value


def split(value):
    high = value.astype(BF16)
    rest = value - high.astype(F32)
    middle = rest.astype(BF16)
    return high, middle, (rest - middle.astype(F32)).astype(BF16)


def turn_out(packed):
    turned = jnp.transpose(packed)
    return jnp.concatenate([turned[:64], turned[64:]], axis=1)


def product(scaled, weights, axis):
    high, middle = (ref[...] for ref in weights)
    over = lambda left, right: lax.dot_general(
        left, right, (((1,), (axis,)), ((), ())), preferred_element_type=F32
    )
    top = over(scaled, high)
    part = over(scaled[:128], middle)
    return top[:64] + (top[64:128] + part[:64]) + (top[128:] + part[64:])


def turn_in(part):
    return jnp.transpose(jnp.concatenate([part[:, :LINE], part[:, LINE:]], axis=0))


def gram_of(turned):
    return lax.dot_general(turned, turned, (((1,), (1,)), ((), ())), precision=HIGH, preferred_element_type=F32)


def inverse_cholesky(gram):
    n = gram.shape[0]
    tiles = []
    sub = lax.broadcasted_iota(jnp.int32, (8, 128), 0)
    lane = lax.broadcasted_iota(jnp.int32, (8, 128), 1)
    for t in range(n // 8):
        eye = jnp.where(lane == sub + 8 * t + n, 1.0, 0.0).astype(F32)
        left = jnp.concatenate([gram[8 * t : 8 * t + 8], jnp.zeros((8, n), F32)], axis=1)
        tiles.append(left + eye)
    scale = [jnp.ones((8, 128), F32) for _ in tiles]
    for top in range(n // 8):
        cols = [
            {t: jnp.broadcast_to(tiles[t][:, 8 * top + j : 8 * top + j + 1], (8, 128)) for t in range(top, n // 8)}
            for j in range(8)
        ]
        for r in range(8):
            pivot = jnp.broadcast_to(cols[r][top][r : r + 1], (8, 128))
            scale[top] = jnp.where(sub == r, lax.rsqrt(pivot), scale[top])
            inv = 1.0 / pivot
            row = jnp.broadcast_to(tiles[top][r : r + 1], (8, 128))
            heads = [jnp.broadcast_to(cols[i][top][r : r + 1], (8, 128)) for i in range(r + 1, 8)]
            for t in range(top, n // 8):
                factor = cols[r][t] * inv
                if t == top:
                    factor = jnp.where(sub > r, factor, 0.0)
                tiles[t] = tiles[t] - factor * row
                for i in range(r + 1, 8):
                    cols[i][t] = cols[i][t] - factor * heads[i - r - 1]
    out = jnp.concatenate([tile * s for tile, s in zip(tiles, scale)], axis=0)
    return out[:, n:]


def near_kernel(points_ref, out_ref):
    points = points_ref[...]
    for i in range(NN):
        out_ref[i] = points


def far_kernel(points_ref, basis_ref, after_ref, out_ref, fold_ref):
    points = points_ref[...]
    for i in range(NF):
        out_ref[i] = points
    fold_ref[...] = fold(basis_ref[...])


def line_of(ref):
    return jnp.concatenate([ref[i, h : h + HALF] for h in (0, HALF) for i in range(ref.shape[0])], axis=0)


def squares(points, rate):
    floats = points.astype(F32)
    return jnp.sum(floats * floats, axis=1, keepdims=True) * rate


def rate_of(width):
    return math.log2(math.e) / (0.25 * width)


def line_kernel(near_ref, rows_ref, squares_ref):
    rows = line_of(near_ref)
    rows_ref[...] = rows
    squares_ref[...] = jnp.broadcast_to(squares(rows, rate_of(rows.shape[1])), squares_ref.shape)


def weights_kernel(own_ref, own_sq_ref, other_ref, other_sq_ref, far_ref, basis_ref, *refs):
    cols = line_of(far_ref)
    count, width = cols.shape
    rate = rate_of(width)
    cols_sq = jnp.transpose(jnp.broadcast_to(squares(cols, rate), (count, 128)))[:1]
    sums = []
    for rows_ref, sq_ref, high_ref, middle_ref in ((own_ref, own_sq_ref, *refs[:2]), (other_ref, other_sq_ref, *refs[2:4])):
        dots = lax.dot_general(rows_ref[...], cols, (((1,), (1,)), ((), ())), preferred_element_type=F32)
        weights = jnp.exp2(dots * (2.0 * rate) - (jnp.tile(sq_ref[...], (1, count // 128)) + cols_sq))
        high = weights.astype(BF16)
        high_ref[...] = high
        middle_ref[...] = (weights - high.astype(F32)).astype(BF16)
        sums.append(jnp.sum(weights, axis=0, keepdims=True))
    sums = sums[0] + sums[1]
    lines = [sums[:, 128 * i : 128 * i + 128] for i in range(count // 128)]
    payload = jnp.concatenate(lines + [jnp.zeros((4, 128), F32), basis_ref[...]], axis=0)
    for i in range(NF):
        refs[4][i] = payload


def first_kernel(*refs):
    own_refs, other_refs = refs[:2], refs[2:4]
    in_ref, part_ref, dinv_ref, rider_ref, deg_ref = refs[4:]
    head = in_ref[0, :8]
    for i in range(1, NF):
        head = head + in_ref[i, :8]
    mine = lax.axis_index(FAR)
    sub = lax.broadcasted_iota(jnp.int32, (8, 128), 0)
    lane = lax.broadcasted_iota(jnp.int32, (8, 128), 1)
    lines = []
    for h in range(2):
        line = jnp.sum(jnp.where(sub == 2 * h + mine // 8, head, 0.0), axis=0, keepdims=True)
        line = pltpu.roll(jnp.broadcast_to(line, (8, 128)), (128 - HALF * (mine % 8)) % 128, 1)
        line = jnp.where(lane < HALF, line, 0.0)
        for shift in (16, 32, 64):
            line = line + pltpu.roll(line, shift, 1)
        lines.append(line)
    deg_ref[...] = jnp.where(lane < HALF, lines[0], lines[1])[0, :OWN]
    rider = lax.rsqrt(jnp.where(sub == 0, lines[0], lines[1]))
    rider_ref[...] = rider
    turned = jnp.transpose(rider)[:HALF]
    first, last = (jnp.broadcast_to(turned[:, h : h + 1], (HALF, 128)) for h in range(2))
    dinv_ref[...] = jnp.where(lax.broadcasted_iota(jnp.int32, (HALF, 128), 1) < 64, first, last)
    inverse = lax.rsqrt(head)
    inverse = jnp.concatenate([inverse[i : i + 1] for i in range(4)], axis=1)
    packed = jnp.concatenate([in_ref[i, 8:] for i in range(NF)], axis=0)
    scaled = jnp.concatenate(split(turn_out(packed) * inverse), axis=0)
    for side, weights in enumerate((own_refs, other_refs)):
        part = turn_in(product(scaled, weights, 1))
        for i in range(NN):
            part_ref[i, HALF * side : HALF * side + HALF] = part[HALF * i : HALF * i + HALF]


def half_kernel(in_ref, dinv_ref, rider_ref, out_ref):
    out_ref[: 2 * HALF] = total(in_ref)
    out_ref[2 * HALF : 3 * HALF] = dinv_ref[...]
    out_ref[3 * HALF :] = rider_ref[...]


def update_kernel(in_ref, out_ref):
    core = lax.axis_index("core")
    mine, other = in_ref[core], in_ref[1 - core]
    sub = lax.broadcasted_iota(jnp.int32, (8, 128), 0)
    payload = jnp.concatenate(
        [
            (mine[:HALF] + other[HALF : 2 * HALF]) * mine[2 * HALF : 3 * HALF],
            (mine[HALF : 2 * HALF] + other[:HALF]) * other[2 * HALF : 3 * HALF],
            jnp.where(sub < 2, mine[3 * HALF :], pltpu.roll(other[3 * HALF :], 2, 0)),
        ],
        axis=0,
    )
    for i in range(NN):
        out_ref[i] = payload


def second_kernel(*refs):
    sides = refs[:2], refs[2:4]
    in_ref, out_ref, gram_ref = refs[4:]
    lane = lax.broadcasted_iota(jnp.int32, (8, 128), 1)
    riders = []
    for v in range(2):
        rider = in_ref[8 * v, 2 * HALF :]
        for i in range(1, 8):
            rider = jnp.where(lane // HALF == i, in_ref[8 * v + i, 2 * HALF :], rider)
        riders.append(rider)
    gram, part = 0.0, 0.0
    for side, weights in enumerate(sides):
        updates = jnp.concatenate([in_ref[i, HALF * side : HALF * side + HALF] for i in range(NN)], axis=0)
        updates = turn_out(updates)
        dinv = [rider[2 * side + h : 2 * side + h + 1] for h in range(2) for rider in riders]
        scaled = jnp.concatenate(split(updates * jnp.concatenate(dinv, axis=1)), axis=0)
        part = part + product(scaled, weights, 0)
        gram = gram + gram_of(updates)
    gram_ref[...] = fold(gram)
    half = gram_ref[pl.ds(pl.multiple_of(lax.axis_index("core") * 16, 16), 16)]
    part = turn_in(part)
    for i in range(NF):
        out_ref[i, :HALF] = part[HALF * i : HALF * i + HALF]
        out_ref[i, HALF:] = half


def collect_kernel(in_ref, dinv_ref, out_ref, gram_ref):
    value = total(in_ref)
    update = value[:HALF] * dinv_ref[...]
    gram_ref[...] = value[HALF:]
    for i in range(NF):
        out_ref[i] = update


def factor_kernel(gram_ref, inverse_ref, both_ref):
    inverse = inverse_cholesky(unfold(jnp.concatenate([gram_ref[0], gram_ref[1]], axis=0)))
    inverse_ref[...] = inverse
    turned = jnp.transpose(inverse)
    none = jnp.zeros_like(turned)
    both_ref[:64] = jnp.concatenate([turned, none], axis=1)
    both_ref[64:] = jnp.concatenate([none, turned], axis=1)


def normalize_kernel(in_ref, inverse_ref, both_ref, update_ref, out_ref):
    turned = turn_out(jnp.concatenate([in_ref[i] for i in range(NF)], axis=0))
    gram = fold(gram_of(jnp.dot(inverse_ref[...], turned, precision=HIGH, preferred_element_type=F32)))
    for i in range(NN):
        out_ref[i] = gram
    mine = in_ref[lax.axis_index(FAR)]
    update_ref[...] = jnp.dot(mine, both_ref[...], precision=HIGH, preferred_element_type=F32)


def relay_kernel(in_ref, out_ref):
    out_ref[...] = total(in_ref)


def final_kernel(in_ref, update_ref, out_ref):
    inverse = inverse_cholesky(unfold(total(in_ref)))
    out_ref[...] = lax.dot_general(
        unfold(update_ref[...]), inverse, (((1,), (1,)), ((), ())), precision=HIGH, preferred_element_type=F32
    )


def per_device(points, basis):
    own, width = points.shape
    shape = lambda *dims, dtype=F32: jax.ShapeDtypeStruct(dims, dtype)
    (near,) = call(near_kernel, [shape(NN, own, width, dtype=BF16)], points, name="near_copies")
    near = exchange(near, NEAR)
    other = swap(near)
    far, basis = call(
        far_kernel,
        [shape(NF, own, width, dtype=BF16), shape(HALF, 128)],
        points,
        basis,
        near,
        specs=[VMEM, VMEM, ANY],
        name="far_copies",
    )
    far = exchange(far, FAR)
    lines = []
    for name, value in (("own", near), ("other", other)):
        lines += call(
            line_kernel, [shape(NN * own, width, dtype=BF16), shape(NN * own, 128)], value, name=name + "_line"
        )
    *weights, sums = call(
        weights_kernel,
        [shape(NN * own, NF * own, dtype=BF16)] * 4 + [shape(NF, 8 + HALF, 128)],
        *lines,
        far,
        basis,
        name="weights",
    )
    part, dinv, rider, degree = call(
        first_kernel,
        [shape(NN, 2 * HALF, 128), shape(HALF, 128), shape(8, 128), shape(own)],
        *weights,
        exchange(sums, FAR),
        name="first_product",
    )
    (part,) = call(half_kernel, [shape(3 * HALF + 8, 128)], exchange(part, NEAR), dinv, rider, name="half_update")
    (update,) = call(update_kernel, [shape(NN, 2 * HALF + 8, 128)], lax.all_gather(part, "core"), name="first_update")
    (part,) = call(
        second_kernel,
        [shape(NF, 2 * HALF, 128)],
        *weights,
        exchange(update, NEAR),
        scratch=[pltpu.VMEM((32, 128), F32)],
        name="second_product",
    )
    update, gram = call(
        collect_kernel, [shape(NF, HALF, 128), shape(16, 128)], exchange(part, FAR), dinv, name="collect"
    )
    everyone = exchange(update, FAR)
    inverses = call(factor_kernel, [shape(64, 64), shape(128, 128)], lax.all_gather(gram, "core"), name="factor")
    update, gram = call(
        normalize_kernel, [shape(HALF, 128), shape(NN, 32, 128)], everyone, *inverses, name="normalize"
    )
    (gram,) = call(relay_kernel, [shape(32, 128)], exchange(gram, NEAR), name="relay")
    (out,) = call(final_kernel, [shape(own, 64)], lax.all_gather(gram, "core"), update, name="orthonormalize")
    return (out, degree)


def solution(mesh):
    fine = Mesh(mesh.devices.reshape(SIZES), AXES)
    return jax.shard_map(
        per_device,
        mesh=fine,
        in_specs=(P(AXES, None), P(AXES, None)),
        out_specs=(P(AXES, None), P(AXES)),
        check_vma=False,
    )
```

```python
import math

import jax
import jax.numpy as jnp
from jax import lax
from jax.experimental import pallas as pl
from jax.experimental.pallas import tpu as pltpu
from jax.sharding import Mesh, PartitionSpec as P

AXES = ("x", "yh", "core", "ym", "yl", "zh", "zl")
SIZES = (4, 2, 2, 2, 2, 4, 2)
NEAR = ("x", "yl", "zl")
FAR = ("yh", "ym", "zh")
NN, NF = 16, 16
OWN, HALF, LINE = 32, 16, 256
HIGH = lax.Precision.HIGHEST
F32, BF16 = jnp.float32, jnp.bfloat16
VMEM = pl.BlockSpec(memory_space=pltpu.VMEM)
ANY = pl.BlockSpec(memory_space=pl.ANY)


def exchange(chunks, axes):
    return lax.all_to_all(chunks, axes, 0, 0, tiled=True)


def swap(value):
    return lax.ppermute(value, "core", [(0, 1), (1, 0)])


def call(body, outs, *args, specs=None, scratch=(), name=None):
    return pl.pallas_call(
        body,
        out_shape=outs,
        in_specs=specs or [VMEM] * len(args),
        out_specs=[VMEM] * len(outs),
        scratch_shapes=list(scratch),
        compiler_params=pltpu.CompilerParams(vmem_limit_bytes=48 * 1024 * 1024),
        name=name,
    )(*args)


def fold(block):
    half = block.shape[0] // 2
    return jnp.concatenate([block[:half], block[half:]], axis=1)


def unfold(packed):
    return jnp.concatenate([packed[:, :64], packed[:, 64:]], axis=0)


def total(ref):
    value = ref[0]
    for i in range(1, ref.shape[0]):
        value = value + ref[i]
    return value


def split(value):
    high = value.astype(BF16)
    rest = value - high.astype(F32)
    middle = rest.astype(BF16)
    return high, middle, (rest - middle.astype(F32)).astype(BF16)


def turn_out(packed):
    turned = jnp.transpose(packed)
    return jnp.concatenate([turned[:64], turned[64:]], axis=1)


def product(scaled, weights, axis):
    high, middle = (ref[...] for ref in weights)
    over = lambda left, right: lax.dot_general(
        left, right, (((1,), (axis,)), ((), ())), preferred_element_type=F32
    )
    top = over(scaled, high)
    part = over(scaled[:128], middle)
    return top[:64] + (top[64:128] + part[:64]) + (top[128:] + part[64:])


def turn_in(part):
    return jnp.transpose(jnp.concatenate([part[:, :LINE], part[:, LINE:]], axis=0))


def gram_of(turned):
    return lax.dot_general(turned, turned, (((1,), (1,)), ((), ())), precision=HIGH, preferred_element_type=F32)


def inverse_cholesky(gram):
    n = gram.shape[0]
    tiles = []
    sub = lax.broadcasted_iota(jnp.int32, (8, 128), 0)
    lane = lax.broadcasted_iota(jnp.int32, (8, 128), 1)
    for t in range(n // 8):
        eye = jnp.where(lane == sub + 8 * t + n, 1.0, 0.0).astype(F32)
        left = jnp.concatenate([gram[8 * t : 8 * t + 8], jnp.zeros((8, n), F32)], axis=1)
        tiles.append(left + eye)
    scale = [jnp.ones((8, 128), F32) for _ in tiles]
    for top in range(n // 8):
        cols = [
            {t: jnp.broadcast_to(tiles[t][:, 8 * top + j : 8 * top + j + 1], (8, 128)) for t in range(top, n // 8)}
            for j in range(8)
        ]
        for r in range(8):
            pivot = jnp.broadcast_to(cols[r][top][r : r + 1], (8, 128))
            scale[top] = jnp.where(sub == r, lax.rsqrt(pivot), scale[top])
            inv = 1.0 / pivot
            row = jnp.broadcast_to(tiles[top][r : r + 1], (8, 128))
            heads = [jnp.broadcast_to(cols[i][top][r : r + 1], (8, 128)) for i in range(r + 1, 8)]
            for t in range(top, n // 8):
                factor = cols[r][t] * inv
                if t == top:
                    factor = jnp.where(sub > r, factor, 0.0)
                tiles[t] = tiles[t] - factor * row
                for i in range(r + 1, 8):
                    cols[i][t] = cols[i][t] - factor * heads[i - r - 1]
    out = jnp.concatenate([tile * s for tile, s in zip(tiles, scale)], axis=0)
    return out[:, n:]


def near_kernel(points_ref, out_ref):
    points = points_ref[...]
    for i in range(NN):
        out_ref[i] = points


def far_kernel(points_ref, basis_ref, after_ref, out_ref, fold_ref):
    points = points_ref[...]
    for i in range(NF):
        out_ref[i] = points
    fold_ref[...] = fold(basis_ref[...])


def line_of(ref):
    return jnp.concatenate([ref[i, h : h + HALF] for h in (0, HALF) for i in range(ref.shape[0])], axis=0)


def squares(points, rate):
    floats = points.astype(F32)
    return jnp.sum(floats * floats, axis=1, keepdims=True) * rate


def rate_of(width):
    return math.log2(math.e) / (0.25 * width)


def line_kernel(near_ref, rows_ref, squares_ref):
    rows = line_of(near_ref)
    rows_ref[...] = rows
    squares_ref[...] = jnp.broadcast_to(squares(rows, rate_of(rows.shape[1])), squares_ref.shape)


def weights_kernel(own_ref, own_sq_ref, other_ref, other_sq_ref, far_ref, basis_ref, *refs):
    cols = line_of(far_ref)
    count, width = cols.shape
    rate = rate_of(width)
    cols_sq = jnp.transpose(jnp.broadcast_to(squares(cols, rate), (count, 128)))[:1]
    sums = []
    for rows_ref, sq_ref, high_ref, middle_ref in ((own_ref, own_sq_ref, *refs[:2]), (other_ref, other_sq_ref, *refs[2:4])):
        dots = lax.dot_general(rows_ref[...], cols, (((1,), (1,)), ((), ())), preferred_element_type=F32)
        weights = jnp.exp2(dots * (2.0 * rate) - (jnp.tile(sq_ref[...], (1, count // 128)) + cols_sq))
        high = weights.astype(BF16)
        high_ref[...] = high
        middle_ref[...] = (weights - high.astype(F32)).astype(BF16)
        sums.append(jnp.sum(weights, axis=0, keepdims=True))
    sums = sums[0] + sums[1]
    lines = [sums[:, 128 * i : 128 * i + 128] for i in range(count // 128)]
    payload = jnp.concatenate(lines + [jnp.zeros((4, 128), F32), basis_ref[...]], axis=0)
    for i in range(NF):
        refs[4][i] = payload


def first_kernel(*refs):
    own_refs, other_refs = refs[:2], refs[2:4]
    in_ref, part_ref, dinv_ref, rider_ref, deg_ref = refs[4:]
    head = in_ref[0, :8]
    for i in range(1, NF):
        head = head + in_ref[i, :8]
    mine = lax.axis_index(FAR)
    sub = lax.broadcasted_iota(jnp.int32, (8, 128), 0)
    lane = lax.broadcasted_iota(jnp.int32, (8, 128), 1)
    lines = []
    for h in range(2):
        line = jnp.sum(jnp.where(sub == 2 * h + mine // 8, head, 0.0), axis=0, keepdims=True)
        line = pltpu.roll(jnp.broadcast_to(line, (8, 128)), (128 - HALF * (mine % 8)) % 128, 1)
        line = jnp.where(lane < HALF, line, 0.0)
        for shift in (16, 32, 64):
            line = line + pltpu.roll(line, shift, 1)
        lines.append(line)
    deg_ref[...] = jnp.where(lane < HALF, lines[0], lines[1])[0, :OWN]
    rider = lax.rsqrt(jnp.where(sub == 0, lines[0], lines[1]))
    rider_ref[...] = rider
    turned = jnp.transpose(rider)[:HALF]
    first, last = (jnp.broadcast_to(turned[:, h : h + 1], (HALF, 128)) for h in range(2))
    dinv_ref[...] = jnp.where(lax.broadcasted_iota(jnp.int32, (HALF, 128), 1) < 64, first, last)
    inverse = lax.rsqrt(head)
    inverse = jnp.concatenate([inverse[i : i + 1] for i in range(4)], axis=1)
    packed = jnp.concatenate([in_ref[i, 8:] for i in range(NF)], axis=0)
    scaled = jnp.concatenate(split(turn_out(packed) * inverse), axis=0)
    for side, weights in enumerate((own_refs, other_refs)):
        part = turn_in(product(scaled, weights, 1))
        for i in range(NN):
            part_ref[i, HALF * side : HALF * side + HALF] = part[HALF * i : HALF * i + HALF]


def half_kernel(in_ref, dinv_ref, rider_ref, out_ref):
    out_ref[: 2 * HALF] = total(in_ref)
    out_ref[2 * HALF : 3 * HALF] = dinv_ref[...]
    out_ref[3 * HALF :] = rider_ref[...]


def update_kernel(in_ref, out_ref):
    core = lax.axis_index("core")
    mine, other = in_ref[core], in_ref[1 - core]
    sub = lax.broadcasted_iota(jnp.int32, (8, 128), 0)
    payload = jnp.concatenate(
        [
            (mine[:HALF] + other[HALF : 2 * HALF]) * mine[2 * HALF : 3 * HALF],
            (mine[HALF : 2 * HALF] + other[:HALF]) * other[2 * HALF : 3 * HALF],
            jnp.where(sub < 2, mine[3 * HALF :], pltpu.roll(other[3 * HALF :], 2, 0)),
        ],
        axis=0,
    )
    for i in range(NN):
        out_ref[i] = payload


def second_kernel(*refs):
    sides = refs[:2], refs[2:4]
    in_ref, out_ref, gram_ref = refs[4:]
    lane = lax.broadcasted_iota(jnp.int32, (8, 128), 1)
    riders = []
    for v in range(2):
        rider = in_ref[8 * v, 2 * HALF :]
        for i in range(1, 8):
            rider = jnp.where(lane // HALF == i, in_ref[8 * v + i, 2 * HALF :], rider)
        riders.append(rider)
    gram, part = 0.0, 0.0
    for side, weights in enumerate(sides):
        updates = jnp.concatenate([in_ref[i, HALF * side : HALF * side + HALF] for i in range(NN)], axis=0)
        updates = turn_out(updates)
        dinv = [rider[2 * side + h : 2 * side + h + 1] for h in range(2) for rider in riders]
        scaled = jnp.concatenate(split(updates * jnp.concatenate(dinv, axis=1)), axis=0)
        part = part + product(scaled, weights, 0)
        gram = gram + gram_of(updates)
    gram_ref[...] = fold(gram)
    half = gram_ref[pl.ds(pl.multiple_of(lax.axis_index("core") * 16, 16), 16)]
    part = turn_in(part)
    for i in range(NF):
        out_ref[i, :HALF] = part[HALF * i : HALF * i + HALF]
        out_ref[i, HALF:] = half


def collect_kernel(in_ref, dinv_ref, out_ref, gram_ref):
    value = total(in_ref)
    update = value[:HALF] * dinv_ref[...]
    gram_ref[...] = value[HALF:]
    for i in range(NF):
        out_ref[i] = update


def factor_kernel(gram_ref, inverse_ref, both_ref):
    inverse = inverse_cholesky(unfold(jnp.concatenate([gram_ref[0], gram_ref[1]], axis=0)))
    inverse_ref[...] = inverse
    turned = jnp.transpose(inverse)
    none = jnp.zeros_like(turned)
    both_ref[:64] = jnp.concatenate([turned, none], axis=1)
    both_ref[64:] = jnp.concatenate([none, turned], axis=1)


def normalize_kernel(in_ref, inverse_ref, both_ref, update_ref, gram_ref):
    turned = turn_out(jnp.concatenate([in_ref[i] for i in range(NF)], axis=0))
    gram_ref[...] = fold(gram_of(jnp.dot(inverse_ref[...], turned, precision=HIGH, preferred_element_type=F32)))
    mine = in_ref[lax.axis_index(FAR)]
    update_ref[...] = jnp.dot(mine, both_ref[...], precision=HIGH, preferred_element_type=F32)


def spread_kernel(in_ref, out_ref):
    gram = total(in_ref)
    for i in range(NN):
        out_ref[i] = gram


def final_kernel(in_ref, update_ref, out_ref):
    inverse = inverse_cholesky(unfold(total(in_ref)))
    out_ref[...] = lax.dot_general(
        unfold(update_ref[...]), inverse, (((1,), (1,)), ((), ())), precision=HIGH, preferred_element_type=F32
    )


def per_device(points, basis):
    own, width = points.shape
    shape = lambda *dims, dtype=F32: jax.ShapeDtypeStruct(dims, dtype)
    (near,) = call(near_kernel, [shape(NN, own, width, dtype=BF16)], points, name="near_copies")
    near = exchange(near, NEAR)
    other = swap(near)
    far, basis = call(
        far_kernel,
        [shape(NF, own, width, dtype=BF16), shape(HALF, 128)],
        points,
        basis,
        near,
        specs=[VMEM, VMEM, ANY],
        name="far_copies",
    )
    far = exchange(far, FAR)
    lines = []
    for name, value in (("own", near), ("other", other)):
        lines += call(
            line_kernel, [shape(NN * own, width, dtype=BF16), shape(NN * own, 128)], value, name=name + "_line"
        )
    *weights, sums = call(
        weights_kernel,
        [shape(NN * own, NF * own, dtype=BF16)] * 4 + [shape(NF, 8 + HALF, 128)],
        *lines,
        far,
        basis,
        name="weights",
    )
    part, dinv, rider, degree = call(
        first_kernel,
        [shape(NN, 2 * HALF, 128), shape(HALF, 128), shape(8, 128), shape(own)],
        *weights,
        exchange(sums, FAR),
        name="first_product",
    )
    (part,) = call(half_kernel, [shape(3 * HALF + 8, 128)], exchange(part, NEAR), dinv, rider, name="half_update")
    (update,) = call(update_kernel, [shape(NN, 2 * HALF + 8, 128)], lax.all_gather(part, "core"), name="first_update")
    (part,) = call(
        second_kernel,
        [shape(NF, 2 * HALF, 128)],
        *weights,
        exchange(update, NEAR),
        scratch=[pltpu.VMEM((32, 128), F32)],
        name="second_product",
    )
    update, gram = call(
        collect_kernel, [shape(NF, HALF, 128), shape(16, 128)], exchange(part, FAR), dinv, name="collect"
    )
    everyone = exchange(update, FAR)
    inverses = call(factor_kernel, [shape(64, 64), shape(128, 128)], lax.all_gather(gram, "core"), name="factor")
    update, gram = call(normalize_kernel, [shape(HALF, 128), shape(32, 128)], everyone, *inverses, name="normalize")
    (gram,) = call(spread_kernel, [shape(NN, 32, 128)], lax.all_gather(gram, "core"), name="spread")
    (out,) = call(final_kernel, [shape(own, 64)], exchange(gram, NEAR), update, name="orthonormalize")
    return (out, degree)


def solution(mesh):
    fine = Mesh(mesh.devices.reshape(SIZES), AXES)
    return jax.shard_map(
        per_device,
        mesh=fine,
        in_specs=(P(AXES, None), P(AXES, None)),
        out_specs=(P(AXES, None), P(AXES)),
        check_vma=False,
    )
```

```python
import math

import jax
import jax.numpy as jnp
from jax import lax
from jax.experimental import pallas as pl
from jax.experimental.pallas import tpu as pltpu
from jax.sharding import Mesh, PartitionSpec as P

AXES = ("x", "yh", "core", "ym", "yl", "zh", "zl")
SIZES = (4, 2, 2, 2, 2, 4, 2)
NEAR = ("x", "yl", "zl")
FAR = ("yh", "ym", "zh")
NN, NF = 16, 16
OWN, HALF, LINE = 32, 16, 256
HIGH = lax.Precision.HIGHEST
F32, BF16 = jnp.float32, jnp.bfloat16
VMEM = pl.BlockSpec(memory_space=pltpu.VMEM)
ANY = pl.BlockSpec(memory_space=pl.ANY)


def exchange(chunks, axes):
    return lax.all_to_all(chunks, axes, 0, 0, tiled=True)


def swap(value):
    return lax.ppermute(value, "core", [(0, 1), (1, 0)])


def call(body, outs, *args, specs=None, scratch=(), name=None):
    return pl.pallas_call(
        body,
        out_shape=outs,
        in_specs=specs or [VMEM] * len(args),
        out_specs=[VMEM] * len(outs),
        scratch_shapes=list(scratch),
        compiler_params=pltpu.CompilerParams(vmem_limit_bytes=48 * 1024 * 1024),
        name=name,
    )(*args)


def fold(block):
    half = block.shape[0] // 2
    return jnp.concatenate([block[:half], block[half:]], axis=1)


def unfold(packed):
    return jnp.concatenate([packed[:, :64], packed[:, 64:]], axis=0)


def total(ref):
    value = ref[0]
    for i in range(1, ref.shape[0]):
        value = value + ref[i]
    return value


def split(value):
    high = value.astype(BF16)
    rest = value - high.astype(F32)
    middle = rest.astype(BF16)
    return high, middle, (rest - middle.astype(F32)).astype(BF16)


def turn_out(packed):
    turned = jnp.transpose(packed)
    return jnp.concatenate([turned[:64], turned[64:]], axis=1)


def product(scaled, weights, axis):
    high, middle = (ref[...] for ref in weights)
    over = lambda left, right: lax.dot_general(
        left, right, (((1,), (axis,)), ((), ())), preferred_element_type=F32
    )
    top = over(scaled, high)
    part = over(scaled[:128], middle)
    return top[:64] + (top[64:128] + part[:64]) + (top[128:] + part[64:])


def turn_in(part):
    return jnp.transpose(jnp.concatenate([part[:, :LINE], part[:, LINE:]], axis=0))


def gram_of(turned):
    return lax.dot_general(turned, turned, (((1,), (1,)), ((), ())), precision=HIGH, preferred_element_type=F32)


def shrink(gram):
    strips = [gram[8 * j : 8 * j + 8, :32] for j in range(4)]
    return jnp.concatenate([fold(gram[32:]), jnp.concatenate(strips, axis=1)], axis=0)


def grow(packed):
    lower = unfold(packed[:16])
    block = jnp.concatenate([packed[16:, 32 * j : 32 * j + 32] for j in range(4)], axis=0)
    upper = jnp.concatenate([block, jnp.transpose(lower)[:32]], axis=1)
    return jnp.concatenate([upper, lower], axis=0)


def inverse_cholesky(gram):
    n = gram.shape[0]
    tiles = []
    sub = lax.broadcasted_iota(jnp.int32, (8, 128), 0)
    lane = lax.broadcasted_iota(jnp.int32, (8, 128), 1)
    for t in range(n // 8):
        eye = jnp.where(lane == sub + 8 * t + n, 1.0, 0.0).astype(F32)
        left = jnp.concatenate([gram[8 * t : 8 * t + 8], jnp.zeros((8, n), F32)], axis=1)
        tiles.append(left + eye)
    scale = [jnp.ones((8, 128), F32) for _ in tiles]
    for top in range(n // 8):
        cols = [
            {t: jnp.broadcast_to(tiles[t][:, 8 * top + j : 8 * top + j + 1], (8, 128)) for t in range(top, n // 8)}
            for j in range(8)
        ]
        for r in range(8):
            pivot = jnp.broadcast_to(cols[r][top][r : r + 1], (8, 128))
            scale[top] = jnp.where(sub == r, lax.rsqrt(pivot), scale[top])
            inv = 1.0 / pivot
            row = jnp.broadcast_to(tiles[top][r : r + 1], (8, 128))
            heads = [jnp.broadcast_to(cols[i][top][r : r + 1], (8, 128)) for i in range(r + 1, 8)]
            for t in range(top, n // 8):
                factor = cols[r][t] * inv
                if t == top:
                    factor = jnp.where(sub > r, factor, 0.0)
                tiles[t] = tiles[t] - factor * row
                for i in range(r + 1, 8):
                    cols[i][t] = cols[i][t] - factor * heads[i - r - 1]
    out = jnp.concatenate([tile * s for tile, s in zip(tiles, scale)], axis=0)
    return out[:, n:]


def near_kernel(points_ref, out_ref):
    points = points_ref[...]
    for i in range(NN):
        out_ref[i] = points


def far_kernel(points_ref, basis_ref, after_ref, out_ref, fold_ref):
    points = points_ref[...]
    for i in range(NF):
        out_ref[i] = points
    fold_ref[...] = fold(basis_ref[...])


def line_of(ref):
    return jnp.concatenate([ref[i, h : h + HALF] for h in (0, HALF) for i in range(ref.shape[0])], axis=0)


def squares(points, rate):
    floats = points.astype(F32)
    return jnp.sum(floats * floats, axis=1, keepdims=True) * rate


def rate_of(width):
    return math.log2(math.e) / (0.25 * width)


def line_kernel(near_ref, rows_ref, squares_ref):
    rows = line_of(near_ref)
    rows_ref[...] = rows
    squares_ref[...] = jnp.broadcast_to(squares(rows, rate_of(rows.shape[1])), squares_ref.shape)


def weights_kernel(own_ref, own_sq_ref, other_ref, other_sq_ref, far_ref, basis_ref, *refs):
    cols = line_of(far_ref)
    count, width = cols.shape
    rate = rate_of(width)
    cols_sq = jnp.transpose(jnp.broadcast_to(squares(cols, rate), (count, 128)))[:1]
    sums = []
    for rows_ref, sq_ref, high_ref, middle_ref in ((own_ref, own_sq_ref, *refs[:2]), (other_ref, other_sq_ref, *refs[2:4])):
        dots = lax.dot_general(rows_ref[...], cols, (((1,), (1,)), ((), ())), preferred_element_type=F32)
        weights = jnp.exp2(dots * (2.0 * rate) - (jnp.tile(sq_ref[...], (1, count // 128)) + cols_sq))
        high = weights.astype(BF16)
        high_ref[...] = high
        middle_ref[...] = (weights - high.astype(F32)).astype(BF16)
        sums.append(jnp.sum(weights, axis=0, keepdims=True))
    sums = sums[0] + sums[1]
    lines = [sums[:, 128 * i : 128 * i + 128] for i in range(count // 128)]
    payload = jnp.concatenate(lines + [jnp.zeros((4, 128), F32), basis_ref[...]], axis=0)
    for i in range(NF):
        refs[4][i] = payload


def first_kernel(*refs):
    own_refs, other_refs = refs[:2], refs[2:4]
    in_ref, part_ref, dinv_ref, rider_ref, deg_ref = refs[4:]
    head = in_ref[0, :8]
    for i in range(1, NF):
        head = head + in_ref[i, :8]
    mine = lax.axis_index(FAR)
    sub = lax.broadcasted_iota(jnp.int32, (8, 128), 0)
    lane = lax.broadcasted_iota(jnp.int32, (8, 128), 1)
    lines = []
    for h in range(2):
        line = jnp.sum(jnp.where(sub == 2 * h + mine // 8, head, 0.0), axis=0, keepdims=True)
        line = pltpu.roll(jnp.broadcast_to(line, (8, 128)), (128 - HALF * (mine % 8)) % 128, 1)
        line = jnp.where(lane < HALF, line, 0.0)
        for shift in (16, 32, 64):
            line = line + pltpu.roll(line, shift, 1)
        lines.append(line)
    deg_ref[...] = jnp.where(lane < HALF, lines[0], lines[1])[0, :OWN]
    rider = lax.rsqrt(jnp.where(sub == 0, lines[0], lines[1]))
    rider_ref[...] = rider
    turned = jnp.transpose(rider)[:HALF]
    first, last = (jnp.broadcast_to(turned[:, h : h + 1], (HALF, 128)) for h in range(2))
    dinv_ref[...] = jnp.where(lax.broadcasted_iota(jnp.int32, (HALF, 128), 1) < 64, first, last)
    inverse = lax.rsqrt(head)
    inverse = jnp.concatenate([inverse[i : i + 1] for i in range(4)], axis=1)
    packed = jnp.concatenate([in_ref[i, 8:] for i in range(NF)], axis=0)
    scaled = jnp.concatenate(split(turn_out(packed) * inverse), axis=0)
    for side, weights in enumerate((own_refs, other_refs)):
        part = turn_in(product(scaled, weights, 1))
        for i in range(NN):
            part_ref[i, HALF * side : HALF * side + HALF] = part[HALF * i : HALF * i + HALF]


def half_kernel(in_ref, dinv_ref, rider_ref, out_ref):
    out_ref[: 2 * HALF] = total(in_ref)
    out_ref[2 * HALF : 3 * HALF] = dinv_ref[...]
    out_ref[3 * HALF :] = rider_ref[...]


def update_kernel(in_ref, out_ref):
    core = lax.axis_index("core")
    mine, other = in_ref[core], in_ref[1 - core]
    sub = lax.broadcasted_iota(jnp.int32, (8, 128), 0)
    payload = jnp.concatenate(
        [
            (mine[:HALF] + other[HALF : 2 * HALF]) * mine[2 * HALF : 3 * HALF],
            (mine[HALF : 2 * HALF] + other[:HALF]) * other[2 * HALF : 3 * HALF],
            jnp.where(sub < 2, mine[3 * HALF :], pltpu.roll(other[3 * HALF :], 2, 0)),
        ],
        axis=0,
    )
    for i in range(NN):
        out_ref[i] = payload


def second_kernel(*refs):
    sides = refs[:2], refs[2:4]
    in_ref, out_ref, gram_ref = refs[4:]
    lane = lax.broadcasted_iota(jnp.int32, (8, 128), 1)
    riders = []
    for v in range(2):
        rider = in_ref[8 * v, 2 * HALF :]
        for i in range(1, 8):
            rider = jnp.where(lane // HALF == i, in_ref[8 * v + i, 2 * HALF :], rider)
        riders.append(rider)
    gram, part = 0.0, 0.0
    for side, weights in enumerate(sides):
        updates = jnp.concatenate([in_ref[i, HALF * side : HALF * side + HALF] for i in range(NN)], axis=0)
        updates = turn_out(updates)
        dinv = [rider[2 * side + h : 2 * side + h + 1] for h in range(2) for rider in riders]
        scaled = jnp.concatenate(split(updates * jnp.concatenate(dinv, axis=1)), axis=0)
        part = part + product(scaled, weights, 0)
        gram = gram + gram_of(updates)
    gram_ref[...] = fold(gram)
    half = gram_ref[pl.ds(pl.multiple_of(lax.axis_index("core") * 16, 16), 16)]
    part = turn_in(part)
    for i in range(NF):
        out_ref[i, :HALF] = part[HALF * i : HALF * i + HALF]
        out_ref[i, HALF:] = half


def collect_kernel(in_ref, dinv_ref, out_ref, gram_ref):
    value = total(in_ref)
    update = value[:HALF] * dinv_ref[...]
    gram_ref[...] = value[HALF:]
    for i in range(NF):
        out_ref[i] = update


def factor_kernel(gram_ref, inverse_ref, both_ref):
    inverse = inverse_cholesky(unfold(jnp.concatenate([gram_ref[0], gram_ref[1]], axis=0)))
    inverse_ref[...] = inverse
    turned = jnp.transpose(inverse)
    none = jnp.zeros_like(turned)
    both_ref[:64] = jnp.concatenate([turned, none], axis=1)
    both_ref[64:] = jnp.concatenate([none, turned], axis=1)


def normalize_kernel(in_ref, inverse_ref, both_ref, update_ref, gram_ref):
    turned = turn_out(jnp.concatenate([in_ref[i] for i in range(NF)], axis=0))
    gram_ref[...] = shrink(gram_of(jnp.dot(inverse_ref[...], turned, precision=HIGH, preferred_element_type=F32)))
    mine = in_ref[lax.axis_index(FAR)]
    update_ref[...] = jnp.dot(mine, both_ref[...], precision=HIGH, preferred_element_type=F32)


def spread_kernel(in_ref, out_ref):
    gram = total(in_ref)
    for i in range(NN):
        out_ref[i] = gram


def final_kernel(in_ref, update_ref, out_ref):
    inverse = inverse_cholesky(grow(total(in_ref)))
    out_ref[...] = lax.dot_general(
        unfold(update_ref[...]), inverse, (((1,), (1,)), ((), ())), precision=HIGH, preferred_element_type=F32
    )


def per_device(points, basis):
    own, width = points.shape
    shape = lambda *dims, dtype=F32: jax.ShapeDtypeStruct(dims, dtype)
    (near,) = call(near_kernel, [shape(NN, own, width, dtype=BF16)], points, name="near_copies")
    near = exchange(near, NEAR)
    other = swap(near)
    far, basis = call(
        far_kernel,
        [shape(NF, own, width, dtype=BF16), shape(HALF, 128)],
        points,
        basis,
        near,
        specs=[VMEM, VMEM, ANY],
        name="far_copies",
    )
    far = exchange(far, FAR)
    lines = []
    for name, value in (("own", near), ("other", other)):
        lines += call(
            line_kernel, [shape(NN * own, width, dtype=BF16), shape(NN * own, 128)], value, name=name + "_line"
        )
    *weights, sums = call(
        weights_kernel,
        [shape(NN * own, NF * own, dtype=BF16)] * 4 + [shape(NF, 8 + HALF, 128)],
        *lines,
        far,
        basis,
        name="weights",
    )
    part, dinv, rider, degree = call(
        first_kernel,
        [shape(NN, 2 * HALF, 128), shape(HALF, 128), shape(8, 128), shape(own)],
        *weights,
        exchange(sums, FAR),
        name="first_product",
    )
    (part,) = call(half_kernel, [shape(3 * HALF + 8, 128)], exchange(part, NEAR), dinv, rider, name="half_update")
    (update,) = call(update_kernel, [shape(NN, 2 * HALF + 8, 128)], lax.all_gather(part, "core"), name="first_update")
    (part,) = call(
        second_kernel,
        [shape(NF, 2 * HALF, 128)],
        *weights,
        exchange(update, NEAR),
        scratch=[pltpu.VMEM((32, 128), F32)],
        name="second_product",
    )
    update, gram = call(
        collect_kernel, [shape(NF, HALF, 128), shape(16, 128)], exchange(part, FAR), dinv, name="collect"
    )
    everyone = exchange(update, FAR)
    inverses = call(factor_kernel, [shape(64, 64), shape(128, 128)], lax.all_gather(gram, "core"), name="factor")
    update, gram = call(normalize_kernel, [shape(HALF, 128), shape(24, 128)], everyone, *inverses, name="normalize")
    (gram,) = call(spread_kernel, [shape(NN, 24, 128)], lax.all_gather(gram, "core"), name="spread")
    (out,) = call(final_kernel, [shape(own, 64)], exchange(gram, NEAR), update, name="orthonormalize")
    return (out, degree)


def solution(mesh):
    fine = Mesh(mesh.devices.reshape(SIZES), AXES)
    return jax.shard_map(
        per_device,
        mesh=fine,
        in_specs=(P(AXES, None), P(AXES, None)),
        out_specs=(P(AXES, None), P(AXES)),
        check_vma=False,
    )
```
